32 devices in a mesh: grp: 4 (over y, core), ctx: 8 (over z, x).
Axes of the slice: x: 2, y: 2, z: 4, core: 2. Of those that a mesh axis runs over, the one named last changes fastest.
Arguments:
- cache: bfloat16 [4, 16384, 576], P('grp', 'ctx'), may hold values from -6 to 6
- queries: bfloat16 [4, 4, 4, 128, 576], P(None, 'grp', None, 'ctx'), may hold values from -72 to 72
- new_latent: bfloat16 [4, 4, 4, 576], P(None, 'grp'), may hold values from -12 to 12
- lengths: int32 [4], replicated, may hold values from 8192 to 16384, as said below
- donor: int32 [4], replicated, may hold values from 0 to 3, as said below
- value_up: bfloat16 [128, 512, 128], P('ctx'), may hold values from -2 to 2
- out_proj: bfloat16 [16384, 7168], P('ctx'), may hold values from -0.0625 to 0.0625
Outputs:
- attn_out: bfloat16 [4, 4, 4, 7168], P(None, 'grp', None, 'ctx')
The draws below stay inside these ranges and needn't reach their ends.
Inputs may be any that keep to these rules, and one draw needn't show every extreme that they name: `lengths`: in every draw some prompt has all 16384 positions valid. `donor`: A slot whose entry is its own index holds a hard prompt; every other entry names such a slot. Slot 3 always holds a hard prompt, and each draw has at least one slot that is not hard.
All inputs are finite; a program needn't handle non-finite values.
Results may differ from the reference program's by a relative error of at most 0.0058.
Values may be sent and summed in bfloat16 or wider, within the bound.
No kernel may reach another device: no remote copies, remote signals or barrier semaphores. Data moves between devices by JAX's collectives and lax.ppermute only.
A program may use at most 128 MiB of HBM per device.

```python
import jax
import jax.numpy as jnp
from jax import lax

D = 7168
HEADS = 128
LATENT = 512
VHEAD = 128
CTX_DEV = 2048
SAMPLES = 4
STEPS = 4
HANDOVER = 3
KEYW = 576
GROUPS = 4
CONTEXT = 16384
N_CTX = 8


def draw_cache(key, part):
    drawn_rows = jnp.clip(jax.random.normal(jax.random.fold_in(key, 11), (GROUPS, CONTEXT, KEYW)), -6.0, 6.0)
    return drawn_rows.astype(jnp.bfloat16)


def draw_queries(key, part):
    draw_shape = (STEPS, GROUPS, SAMPLES, HEADS, KEYW)
    drawn_rows = jnp.clip(1.5 * jax.random.normal(jax.random.fold_in(key, 12), draw_shape), -6.0, 6.0)
    return drawn_rows.astype(jnp.bfloat16)


def draw_lengths(key, part):
    spread = jax.random.randint(jax.random.fold_in(key, 21), (GROUPS,), CONTEXT // 2, CONTEXT + 1)
    full_group = jax.random.randint(jax.random.fold_in(key, 22), (), 0, GROUPS)
    return jnp.where(jnp.arange(GROUPS) == full_group, CONTEXT, spread).astype(jnp.int32)


def draw_donor(key, part):
    rest_order = jax.random.permutation(jax.random.fold_in(key, 31), GROUPS - 1).astype(jnp.int32)
    shuffled = jnp.concatenate([jnp.full((1,), GROUPS - 1, jnp.int32), rest_order])
    hard_count = jax.random.randint(jax.random.fold_in(key, 32), (), 1, GROUPS)
    position = jnp.argsort(shuffled, stable=True)
    chosen = jax.random.randint(jax.random.fold_in(key, 33), (GROUPS,), 0, hard_count)
    return jnp.where(position < hard_count, jnp.arange(GROUPS), shuffled[chosen]).astype(jnp.int32)


def raised(result, rng, source, target, blocks, factor):
    def block_of(axis_at):
        return (jnp.arange(result.shape[axis_at]) // (result.shape[axis_at] // blocks)).reshape((-1,) + (1,) * (result.ndim - 1 - axis_at))

    one_side = jax.random.permutation(rng, blocks)[block_of(target)]
    second = (block_of(target) + blocks // 2) % blocks
    return jnp.where((block_of(source) == one_side) | (block_of(source) == second), factor * result, result)


def levels(key, dims, split, smallest, largest):
    def one(axis_at, shards_of):
        steps = jax.random.uniform(jax.random.fold_in(jax.random.fold_in(key, 6), axis_at), (shards_of,), jnp.float32, smallest / len(split), largest / len(split))
        return jnp.repeat(jnp.exp(steps), dims[axis_at] // shards_of).reshape((-1,) + (1,) * (len(dims) - axis_at - 1))

    level = one(*split[0])
    for cut in split[1:]:
        level = level * one(*cut)
    return level


def scatter_about(rng, shape, scale, bound, pieces=(), kind=jnp.bfloat16):
    gain = levels(rng, shape, pieces, -0.22, 0.18) if pieces else 1.0
    entries = jax.random.normal(rng, shape, jnp.float32) * scale * gain
    return jnp.minimum(jnp.maximum(entries, -bound), bound).astype(kind)


def noise_with(stream_key, shape, deviation, most, pieces, heavy, held_as=jnp.bfloat16):
    values = deviation * jax.random.normal(stream_key, shape, jnp.float32)
    if pieces:
        values = values * levels(stream_key, shape, pieces, -0.22, 0.18)
    return jnp.clip(raised(values, jax.random.fold_in(stream_key, 3), *heavy), -most, most).astype(held_as)


def setup_inputs(seed: int = 0) -> dict:
    arg_keys = jax.random.split(jax.random.key(seed), 8)
    return {
        "cache": draw_cache(jax.random.fold_in(arg_keys[7], 71), 0),
        "queries": draw_queries(jax.random.fold_in(arg_keys[7], 71), 0),
        "new_latent": scatter_about(arg_keys[2], (STEPS, GROUPS, SAMPLES, KEYW), 2.0, 12.0, ((1, 4),)),
        "lengths": draw_lengths(jax.random.fold_in(arg_keys[7], 71), 0),
        "donor": draw_donor(jax.random.fold_in(arg_keys[7], 71), 0),
        "value_up": scatter_about(arg_keys[5], (HEADS, LATENT, VHEAD), 0.35, 2.0, ((0, 8),)),
        "out_proj": noise_with(arg_keys[6], (HEADS * VHEAD, D), (HEADS * VHEAD) ** -0.5, 0.0625, ((0, 8),), (0, 1, 8, 2.0)),
    }


score_scale = 192.0 ** -0.5
far_below = -1e30


def block_partial(query_rows, cache_rows, valid_mask):
    logits = jnp.dot(query_rows, cache_rows.T, preferred_element_type=jnp.float32) * score_scale
    logits = jnp.where(valid_mask[None, :], logits, far_below)
    top_score = jnp.max(logits, axis=1)
    weights = jnp.where(valid_mask[None, :], jnp.exp(logits - top_score[:, None]), 0.0)
    weight_sum = jnp.sum(weights, axis=1)
    partial_out = jnp.dot(weights.astype(jnp.bfloat16), cache_rows[:, :LATENT], preferred_element_type=jnp.float32)
    return top_score, weight_sum, partial_out


def combine(earlier, later):
    top_score = jnp.maximum(earlier[0], later[0])
    scale_one = jnp.exp(earlier[0] - top_score)
    scale_two = jnp.exp(later[0] - top_score)
    return (top_score, earlier[1] * scale_one + later[1] * scale_two,
            earlier[2] * scale_one[..., None] + later[2] * scale_two[..., None])


def reference(cache, queries, new_latent, lengths, donor, value_up, out_proj):
    row_count = SAMPLES * HEADS
    highest = lax.Precision.HIGHEST
    step_outs = []
    for step_index in range(STEPS):
        group_outs = []
        for group_index in range(GROUPS):
            if step_index < HANDOVER:
                prompt_rows = cache[group_index]
                prompt_len = lengths[group_index]
            else:
                prompt_rows = lax.dynamic_index_in_dim(cache, donor[group_index], 0, keepdims=False)
                prompt_len = lax.dynamic_index_in_dim(lengths, donor[group_index], 0, keepdims=False)
            query_rows = queries[step_index, group_index].reshape(row_count, KEYW)

            def visit(carried, block_no):
                offset_at = (block_no * CTX_DEV).astype(jnp.int32)
                cache_block = lax.dynamic_slice_in_dim(prompt_rows, offset_at, CTX_DEV, 0)
                valid_mask = offset_at + jnp.arange(CTX_DEV, dtype=jnp.int32) < prompt_len
                return combine(carried, block_partial(query_rows, cache_block, valid_mask)), None

            initial = (jnp.full((row_count,), far_below, jnp.float32), jnp.zeros((row_count,), jnp.float32),
                       jnp.zeros((row_count, LATENT), jnp.float32))
            merged, _ = lax.scan(visit, initial, jnp.arange(N_CTX, dtype=jnp.int32))
            merged = (merged[0].reshape(SAMPLES, HEADS), merged[1].reshape(SAMPLES, HEADS),
                      merged[2].reshape(SAMPLES, HEADS, LATENT))
            fresh_keys = new_latent[:step_index + 1, group_index].astype(jnp.float32)
            query_wide = queries[step_index, group_index].astype(jnp.float32)
            fresh_logits = jnp.einsum('shc,tsc->sht', query_wide, fresh_keys, precision=highest) * score_scale
            fresh_top = jnp.max(fresh_logits, axis=2)
            fresh_weights = jnp.exp(fresh_logits - fresh_top[..., None])
            fresh_sum = jnp.sum(fresh_weights, axis=2)
            fresh_part = jnp.einsum('sht,tsl->shl', fresh_weights, fresh_keys[..., :LATENT], precision=highest)
            merged = combine(merged, (fresh_top, fresh_sum, fresh_part))
            attended = (merged[2] / merged[1][..., None]).astype(jnp.bfloat16)
            head_values = jnp.einsum('shl,hlv->shv', attended.astype(jnp.float32), value_up.astype(jnp.float32),
                                     precision=highest).astype(jnp.bfloat16)
            mixed_out = jnp.dot(head_values.reshape(SAMPLES, HEADS * VHEAD), out_proj,
                                preferred_element_type=jnp.float32).astype(jnp.bfloat16)
            group_outs.append(mixed_out)
        step_outs.append(jnp.stack(group_outs))
    return jnp.stack(step_outs)
```

```python
import functools

import jax
import jax.numpy as jnp
from jax import lax
from jax.experimental import pallas as pl
from jax.experimental.pallas import tpu as pltpu
from jax.sharding import PartitionSpec as P

HANDOVER = 3
EXTRA = 16
MIB = 1 << 20

score_scale = 192.0 ** (-0.5)
far_below = -1e30

ROWS_BY_ROWS = (((1,), (1,)), ((), ()))


def diagonal(n):
    return lax.broadcasted_iota(jnp.int32, (n, n), 0) == lax.broadcasted_iota(jnp.int32, (n, n), 1)


def to_row(column):
    n = column.shape[0]
    return jnp.sum(jnp.where(diagonal(n), column, 0.0), axis=0, keepdims=True)


def to_column(row):
    n = row.shape[1]
    return jnp.sum(jnp.where(diagonal(n), row, 0.0), axis=1, keepdims=True)


def split_three(value):
    high = value.astype(jnp.bfloat16).astype(jnp.float32)
    rest = value - high
    middle = rest.astype(jnp.bfloat16).astype(jnp.float32)
    return high, middle, rest - middle


def store_packed(out_ref, part, peak_row, total_row):
    rows, width = part.shape
    out_ref[0:rows, :] = part.astype(jnp.bfloat16)
    line = lax.broadcasted_iota(jnp.int32, (EXTRA, rows), 0)
    block = jnp.zeros((EXTRA, rows), jnp.float32)
    for at, piece in enumerate(split_three(peak_row) + split_three(total_row)):
        block = jnp.where(line == at, piece, block)
    if rows < width:
        out_ref[rows : rows + EXTRA, :] = jnp.zeros((EXTRA, width), jnp.bfloat16)
    out_ref[rows : rows + EXTRA, 0:rows] = block.astype(jnp.bfloat16)


def load_packed(ref):
    rows = ref.shape[0] - EXTRA
    block = ref[rows : rows + EXTRA, 0:rows].astype(jnp.float32)
    peak = block[0:1] + block[1:2] + block[2:3]
    total = block[3:4] + block[4:5] + block[5:6]
    return peak, total, ref[0:rows, :].astype(jnp.float32)


def attend_block(query, cache_ref, limit, score_ref, latent):
    rows = query.shape[0]
    length = cache_ref.shape[0]
    tile = min(512, length)
    peak = jnp.full((rows, 1), far_below, jnp.float32)
    for start in range(0, length, tile):
        scores = (
            lax.dot_general(
                query,
                cache_ref[start : start + tile, :],
                ROWS_BY_ROWS,
                preferred_element_type=jnp.float32,
            )
            * score_scale
        )
        position = start + lax.broadcasted_iota(jnp.int32, (1, tile), 1)
        scores = jnp.where(position < limit, scores, far_below)
        score_ref[0:rows, start : start + tile] = scores
        peak = jnp.maximum(peak, jnp.max(scores, axis=1, keepdims=True))
    total = jnp.zeros((rows, 1), jnp.float32)
    part = jnp.zeros((rows, latent), jnp.float32)
    for start in range(0, length, tile):
        weights = jnp.exp(score_ref[0:rows, start : start + tile] - peak)
        total = total + jnp.sum(weights, axis=1, keepdims=True)
        part = part + jnp.dot(
            weights.astype(jnp.bfloat16),
            cache_ref[start : start + tile, 0:latent],
            preferred_element_type=jnp.float32,
        )
    some = limit > 0
    return peak, jnp.where(some, total, 0.0), jnp.where(some, part, 0.0)


def fresh_block(query, fresh, first_step, samples, heads, latent):
    rows, columns = query.shape[0], fresh.shape[0]
    scores = (
        lax.dot_general(query, fresh, ROWS_BY_ROWS, preferred_element_type=jnp.float32)
        * score_scale
    )
    row = lax.broadcasted_iota(jnp.int32, (rows, columns), 0) // heads
    column = lax.broadcasted_iota(jnp.int32, (rows, columns), 1)
    seen = (column % samples == row % samples) & (column // samples <= row // samples + first_step)
    scores = jnp.where(seen, scores, far_below)
    peak = jnp.max(scores, axis=1, keepdims=True)
    weights = jnp.where(seen, jnp.exp(scores - peak), 0.0)
    total = jnp.sum(weights, axis=1, keepdims=True)
    part = jnp.dot(
        weights,
        fresh[:, 0:latent].astype(jnp.float32),
        precision=lax.Precision.HIGHEST,
        preferred_element_type=jnp.float32,
    )
    return peak, total, part


def attend_kernel(kinds, latent, fresh_info, *refs):
    count = len(kinds)
    limit_ref, cache_ref = refs[0], refs[1]
    queries = refs[2 : 2 + count]
    rest = list(refs[2 + count :])
    fresh_ref = rest.pop(0) if fresh_info else None
    score_ref = rest.pop()
    limit = limit_ref[0]
    for kind, query_ref in zip(kinds, queries):
        query = query_ref[...]
        peak, total, part = attend_block(query, cache_ref, limit, score_ref, latent)
        if kind == "own":
            other = fresh_block(query, fresh_ref[...], *fresh_info, latent)
            top = jnp.maximum(peak, other[0])
            one, two = jnp.exp(peak - top), jnp.exp(other[0] - top)
            total = total * one + other[1] * two
            part = part * one + other[2] * two
            peak = top
        peak_row, total_row = to_row(peak), to_row(total)
        if kind == "send":
            store_packed(rest.pop(0), part, peak_row, total_row)
        else:
            rest.pop(0)[...] = part
            stats_ref = rest.pop(0)
            line = lax.broadcasted_iota(jnp.int32, stats_ref.shape, 0)
            stats_ref[...] = jnp.where(line == 0, peak_row, total_row)


def whole(memory=pltpu.VMEM):
    return pl.BlockSpec(memory_space=memory)


def attend(kinds, queries, cache_rows, limit, latent, fresh=None, fresh_info=None):
    out_shape = []
    flops = 0
    for kind, query in zip(kinds, queries):
        rows = query.shape[0]
        flops += 2 * rows * cache_rows.shape[0] * (cache_rows.shape[1] + latent)
        if kind == "send":
            out_shape.append(jax.ShapeDtypeStruct((rows + EXTRA, latent), jnp.bfloat16))
        else:
            out_shape.append(jax.ShapeDtypeStruct((rows, latent), jnp.float32))
            out_shape.append(jax.ShapeDtypeStruct((8, rows), jnp.float32))
    most = max(query.shape[0] for query in queries)
    operands = [limit, cache_rows, *queries] + ([fresh] if fresh_info else [])
    outs = pl.pallas_call(
        functools.partial(attend_kernel, tuple(kinds), latent, fresh_info),
        out_shape=out_shape,
        in_specs=[whole(pltpu.SMEM)] + [whole()] * (len(operands) - 1),
        out_specs=[whole()] * len(out_shape),
        scratch_shapes=[pltpu.VMEM((most, cache_rows.shape[0]), jnp.float32)],
        compiler_params=pltpu.CompilerParams(vmem_limit_bytes=24 * MIB),
        cost_estimate=pl.CostEstimate(
            flops=flops, bytes_accessed=4 * MIB, transcendentals=flops // 2200
        ),
        name="attend_" + "_".join(kinds),
    )(*operands)
    outs = list(outs)
    results = []
    for kind in kinds:
        if kind == "send":
            results.append(outs.pop(0))
        else:
            results.append((outs.pop(0), outs.pop(0)))
    return results


def merge_kernel(count, *refs):
    for at in range(count):
        packed_ref, part_ref, stats_ref = refs[3 * at : 3 * at + 3]
        out_ref = refs[3 * count + at]
        peak, total, part = load_packed(packed_ref)
        own_peak, own_total = stats_ref[0:1, :], stats_ref[1:2, :]
        top = jnp.maximum(peak, own_peak)
        one, two = jnp.exp(peak - top), jnp.exp(own_peak - top)
        merged = part * to_column(one) + part_ref[...] * to_column(two)
        store_packed(out_ref, merged, top, total * one + own_total * two)


def merge(pairs):
    operands = []
    for packed, (part, stats) in pairs:
        operands += [packed, part, stats]
    return pl.pallas_call(
        functools.partial(merge_kernel, len(pairs)),
        out_shape=[jax.ShapeDtypeStruct(packed.shape, packed.dtype) for packed, _ in pairs],
        in_specs=[whole()] * len(operands),
        out_specs=[whole()] * len(pairs),
        compiler_params=pltpu.CompilerParams(vmem_limit_bytes=16 * MIB),
        cost_estimate=pl.CostEstimate(flops=1 << 20, bytes_accessed=2 * MIB, transcendentals=1024),
        name="merge",
    )(*operands)


def finish_kernel(chunks, heads, *refs):
    value_ref, out_ref, rows_ref = refs[-3:]
    lanes = rows_ref.shape[0]
    at = 0
    for index in range(chunks):
        left_ref, right_ref, part_ref, stats_ref = refs[4 * index : 4 * index + 4]
        left, right = load_packed(left_ref), load_packed(right_ref)
        own_peak, own_total = stats_ref[0:1, :], stats_ref[1:2, :]
        top = jnp.maximum(jnp.maximum(left[0], right[0]), own_peak)
        one, two, three = jnp.exp(left[0] - top), jnp.exp(right[0] - top), jnp.exp(own_peak - top)
        total = left[1] * one + right[1] * two + own_total * three
        merged = left[2] * to_column(one) + right[2] * to_column(two)
        merged = (merged + part_ref[...] * to_column(three)) / to_column(total)
        rows = merged.shape[0]
        for lane in range(lanes):
            rows_ref[lane, at : at + rows, :] = merged[:, lane * 128 : (lane + 1) * 128]
        at += rows
    width = value_ref.shape[2]
    for head in range(heads):
        picked = pl.ds(head, at // heads, stride=heads)
        attended = jnp.concatenate([rows_ref[lane, picked, :] for lane in range(lanes)], axis=1)
        attended = attended.astype(jnp.bfloat16)
        values = jnp.dot(attended, value_ref[head], preferred_element_type=jnp.float32)
        out_ref[:, head * width : (head + 1) * width] = values.astype(jnp.bfloat16)


def finish(chunk_parts, value_up):
    heads, latent, width = value_up.shape
    operands = []
    rows = 0
    for left, right, (part, stats) in chunk_parts:
        operands += [left, right, part, stats]
        rows += part.shape[0]
    operands.append(value_up)
    return pl.pallas_call(
        functools.partial(finish_kernel, len(chunk_parts), heads),
        out_shape=jax.ShapeDtypeStruct((rows // heads, heads * width), jnp.bfloat16),
        in_specs=[whole()] * len(operands),
        out_specs=whole(),
        scratch_shapes=[pltpu.VMEM((latent // 128, rows, 128), jnp.float32)],
        compiler_params=pltpu.CompilerParams(vmem_limit_bytes=16 * MIB),
        cost_estimate=pl.CostEstimate(flops=1 << 24, bytes_accessed=4 * MIB, transcendentals=1024),
        name="finish",
    )(*operands)


def project_kernel(values_ref, weight_ref, out_ref):
    out_ref[...] = jnp.dot(
        values_ref[...], weight_ref[...], preferred_element_type=jnp.float32
    ).astype(out_ref.dtype)


def project(values, out_proj, parts):
    rows, depth = values.shape
    width = out_proj.shape[1]
    share = width // parts
    cost = pl.CostEstimate(
        flops=2 * rows * depth * width, bytes_accessed=2 * depth * width, transcendentals=0
    )
    params = pltpu.CompilerParams(
        vmem_limit_bytes=24 * MIB, dimension_semantics=("arbitrary",)
    )
    tile = share
    while share % 128 and tile % 128:
        tile *= 2
    shared = share % 128 == 0
    if shared:
        out_shape = jax.ShapeDtypeStruct((parts, rows, share), jnp.bfloat16)
        out_spec = pl.BlockSpec((None, rows, share), lambda j: (j, 0, 0))
    else:
        out_shape = jax.ShapeDtypeStruct((rows, width), jnp.bfloat16)
        out_spec = pl.BlockSpec((rows, tile), lambda j: (0, j))
    out = pl.pallas_call(
        project_kernel,
        grid=(width // tile,),
        out_shape=out_shape,
        in_specs=[
            pl.BlockSpec((rows, depth), lambda j: (0, 0)),
            pl.BlockSpec((depth, tile), lambda j: (0, j)),
        ],
        out_specs=out_spec,
        compiler_params=params,
        cost_estimate=cost,
        name="project",
    )(values, out_proj)
    if not shared:
        out = out.reshape(rows, parts, share).transpose(1, 0, 2)
    return out


def handed_over(cache_rows, donor, my_group, group_count):
    source = jnp.sum(jnp.where(lax.iota(jnp.int32, group_count) == my_group, donor, 0))

    def gather_all():
        shards = lax.all_gather(cache_rows, "grp", axis=0, tiled=False)
        return lax.dynamic_index_in_dim(shards, source, 0, keepdims=False)

    if group_count != 4:
        return source, gather_all()
    half = cache_rows.shape[0] // 2
    core, plane = my_group % 2, my_group // 2
    core_swap = [(g, g ^ 1) for g in range(4)]
    plane_swap = [(g, g ^ 2) for g in range(4)]
    beside = lax.ppermute(cache_rows, "grp", core_swap)
    wanted, crowded = [], []
    for at in range(2):
        first, second = donor[2 * at], donor[2 * at + 1]
        first_far, second_far = first // 2 != at, second // 2 != at
        wanted.append(jnp.where(first_far, first, second))
        crowded.append(first_far & second_far & (first != second))
    asked = jnp.where(plane == 0, wanted[1], wanted[0])
    offered = jnp.where(
        asked % 2 == core,
        lax.dynamic_slice_in_dim(cache_rows, core * half, half, 0),
        lax.dynamic_slice_in_dim(beside, core * half, half, 0),
    )
    mine = lax.ppermute(offered, "grp", plane_swap)
    other = lax.ppermute(mine, "grp", core_swap)
    far_rows = jnp.concatenate(
        [jnp.where(core == 0, mine, other), jnp.where(core == 0, other, mine)]
    )
    near_rows = jnp.where(source == my_group, cache_rows, beside)
    rows = jnp.where(source // 2 == plane, near_rows, far_rows)
    rows = lax.cond(crowded[0] | crowded[1], gather_all, lambda: rows)
    return source, rows


def body(cache, queries, new_latent, lengths, donor, value_up, out_proj):
    my_group = lax.axis_index("grp")
    group_count = lax.axis_size("grp")
    parts = lax.axis_size("ctx")
    steps, _, samples, heads, key_width = queries.shape
    latent = value_up.shape[1]
    own_rows = cache[0]
    local_len = own_rows.shape[0]
    first = lax.axis_index("ctx") * local_len
    labels = lax.iota(jnp.int32, group_count)

    def limit_of(group):
        length = jnp.sum(jnp.where(labels == group, lengths, 0))
        return jnp.clip(length - first, 0, local_len).astype(jnp.int32)[None]

    source, moved_rows = handed_over(own_rows, donor, my_group, group_count)
    fresh = new_latent.reshape(steps * samples, key_width)

    ring = list(range(0, parts, 2)) + list(range(parts - 1, 0, -2))
    to_right = [(ring[i], ring[(i + 1) % parts]) for i in range(parts)]
    to_left = [(b, a) for a, b in to_right]
    right = functools.partial(lax.ppermute, axis_name="ctx", perm=to_right)
    left = functools.partial(lax.ppermute, axis_name="ctx", perm=to_left)
    reach = parts // 2

    query_rows = queries.reshape(steps, samples * heads, key_width)
    chunks = [
        (0, query_rows[:HANDOVER].reshape(-1, key_width), own_rows, limit_of(my_group)),
        (HANDOVER, query_rows[HANDOVER:].reshape(-1, key_width), moved_rows, limit_of(source)),
    ]
    gathered = []
    for _, own_query, _, _ in chunks:
        from_left, from_right = [own_query], [own_query]
        for hop in range(1, reach + 1):
            from_left.append(right(from_left[-1]))
            if hop < reach:
                from_right.append(left(from_right[-1]))
        gathered.append((from_left, from_right))
    finals = []
    for (first_step, own_query, rows, limit), (from_left, from_right) in zip(chunks, gathered):
        fresh_info = (first_step, samples, heads)
        (own_part,) = attend(["own"], [own_query], rows, limit, latent, fresh, fresh_info)
        part_left, part_right = {}, {}
        for hop in range(1, reach + 1):
            todo = [(part_left, from_left, "send" if hop == reach else "keep")]
            if hop < reach:
                todo.append((part_right, from_right, "send" if hop == reach - 1 else "keep"))
            results = attend(
                [kind for _, _, kind in todo], [q[hop] for _, q, _ in todo], rows, limit, latent
            )
            for (store, _, _), result in zip(todo, results):
                store[hop] = result
        going_left, going_right = part_left[reach], None
        for hop in range(reach, 0, -1):
            came = left(going_left)
            if hop == reach:
                going_right = part_right[reach - 1]
                going_left = merge([(came, part_left[hop - 1])])[0]
                continue
            came_right = right(going_right)
            if hop > 1:
                going_left, going_right = merge(
                    [(came, part_left[hop - 1]), (came_right, part_right[hop - 1])]
                )
            else:
                finals.append((came, came_right, own_part))
    head_values = finish(finals, value_up)
    term = project(head_values, out_proj, parts)
    shares = lax.all_to_all(term, "ctx", split_axis=0, concat_axis=0, tiled=True)
    mixed = jnp.sum(shares.astype(jnp.float32), axis=0).astype(jnp.bfloat16)
    return mixed.reshape(steps, 1, samples, mixed.shape[-1])


def solution(mesh):
    return jax.shard_map(
        body,
        mesh=mesh,
        in_specs=(
            P("grp", "ctx", None),
            P(None, "grp", None, "ctx", None),
            P(None, "grp", None, None),
            P(),
            P(),
            P("ctx", None, None),
            P("ctx", None),
        ),
        out_specs=P(None, "grp", None, "ctx"),
        check_vma=False,
    )
```

```python
import functools

import jax
import jax.numpy as jnp
from jax import lax
from jax.experimental import pallas as pl
from jax.experimental.pallas import tpu as pltpu
from jax.sharding import PartitionSpec as P

HANDOVER = 3
EXTRA = 16
MIB = 1 << 20

score_scale = 192.0 ** (-0.5)
far_below = -1e30

ROWS_BY_ROWS = (((1,), (1,)), ((), ()))


def diagonal(n):
    return lax.broadcasted_iota(jnp.int32, (n, n), 0) == lax.broadcasted_iota(jnp.int32, (n, n), 1)


def to_row(column):
    n = column.shape[0]
    return jnp.sum(jnp.where(diagonal(n), column, 0.0), axis=0, keepdims=True)


def to_column(row):
    n = row.shape[1]
    return jnp.sum(jnp.where(diagonal(n), row, 0.0), axis=1, keepdims=True)


def split_three(value):
    high = value.astype(jnp.bfloat16).astype(jnp.float32)
    rest = value - high
    middle = rest.astype(jnp.bfloat16).astype(jnp.float32)
    return high, middle, rest - middle


def sections_of(rows):
    return 2 if rows % 32 == 0 else 1


def store_packed(out_ref, sections):
    rows, width = sections[0][0].shape
    end = rows * len(sections)
    line = lax.broadcasted_iota(jnp.int32, (EXTRA, rows), 0)
    block = jnp.zeros((EXTRA, rows), jnp.float32)
    for at, (part, peak, total) in enumerate(sections):
        out_ref[at * rows : (at + 1) * rows, :] = part.astype(jnp.bfloat16)
        for index, piece in enumerate(split_three(peak) + split_three(total)):
            block = jnp.where(line == 6 * at + index, piece, block)
    if rows < width:
        out_ref[end : end + EXTRA, :] = jnp.zeros((EXTRA, width), jnp.bfloat16)
    out_ref[end : end + EXTRA, 0:rows] = block.astype(jnp.bfloat16)


def load_packed(ref, rows, at):
    end = ref.shape[0] - EXTRA
    block = ref[end : end + EXTRA, 0:rows].astype(jnp.float32)
    line = [block[6 * at + i : 6 * at + i + 1] for i in range(6)]
    part = ref[at * rows : (at + 1) * rows, :].astype(jnp.float32)
    return part, line[0] + line[1] + line[2], line[3] + line[4] + line[5]


def load_kept(part_ref, stats_ref, at):
    rows = stats_ref.shape[1]
    part = part_ref[at * rows : (at + 1) * rows, :]
    return part, stats_ref[2 * at : 2 * at + 1, :], stats_ref[2 * at + 1 : 2 * at + 2, :]


def combine(*parts):
    peak = functools.reduce(jnp.maximum, [part[1] for part in parts])
    factors = [jnp.exp(part[1] - peak) for part in parts]
    total = sum(part[2] * factor for part, factor in zip(parts, factors))
    merged = sum(part[0] * to_column(factor) for part, factor in zip(parts, factors))
    return merged, peak, total


def attend_block(query, cache_ref, limit, score_ref, latent):
    rows = query.shape[0]
    length = cache_ref.shape[1]
    tile = min(512, length)
    peak = jnp.full((rows, 1), far_below, jnp.float32)
    for start in range(0, length, tile):
        scores = (
            jnp.dot(
                query, cache_ref[:, start : start + tile], preferred_element_type=jnp.float32
            )
            * score_scale
        )
        position = start + lax.broadcasted_iota(jnp.int32, (1, tile), 1)
        scores = jnp.where(position < limit, scores, far_below)
        score_ref[0:rows, start : start + tile] = scores
        peak = jnp.maximum(peak, jnp.max(scores, axis=1, keepdims=True))
    total = jnp.zeros((rows, 1), jnp.float32)
    part = jnp.zeros((rows, latent), jnp.float32)
    for start in range(0, length, tile):
        weights = jnp.exp(score_ref[0:rows, start : start + tile] - peak)
        total = total + jnp.sum(weights, axis=1, keepdims=True)
        part = part + lax.dot_general(
            weights.astype(jnp.bfloat16),
            cache_ref[0:latent, start : start + tile],
            ROWS_BY_ROWS,
            preferred_element_type=jnp.float32,
        )
    some = limit > 0
    return peak, jnp.where(some, total, 0.0), jnp.where(some, part, 0.0)


def fresh_block(query, fresh_ref, rows_ref, first_step, heads, latent):
    steps, samples, _ = fresh_ref.shape
    for step in range(steps):
        rows_ref[step * samples : (step + 1) * samples, :] = fresh_ref[step].astype(jnp.float32)
    fresh = rows_ref[...].astype(jnp.bfloat16)
    rows, columns = query.shape[0], fresh.shape[0]
    scores = (
        lax.dot_general(query, fresh, ROWS_BY_ROWS, preferred_element_type=jnp.float32)
        * score_scale
    )
    row = lax.broadcasted_iota(jnp.int32, (rows, columns), 0) // heads
    column = lax.broadcasted_iota(jnp.int32, (rows, columns), 1)
    seen = (column % samples == row % samples) & (column // samples <= row // samples + first_step)
    scores = jnp.where(seen, scores, far_below)
    peak = jnp.max(scores, axis=1, keepdims=True)
    weights = jnp.where(seen, jnp.exp(scores - peak), 0.0)
    total = jnp.sum(weights, axis=1, keepdims=True)
    part = jnp.dot(
        weights,
        rows_ref[:, 0:latent],
        precision=lax.Precision.HIGHEST,
        preferred_element_type=jnp.float32,
    )
    return peak, total, part


def fetch_rows(info_ref, near, halves, cache_ref, sem):
    me, source = info_ref[2], info_ref[3]
    half = halves[0].shape[0]

    def whole_copy(ref):
        copy = pltpu.make_async_copy(ref, cache_ref, sem.at[0])
        copy.start()
        copy.wait()

    @pl.when(source == me)
    def _():
        whole_copy(near[0])

    @pl.when((source != me) & ((source >> 1) == (me >> 1)))
    def _():
        whole_copy(near[1])

    @pl.when((source >> 1) != (me >> 1))
    def _():
        core = me & 1
        copies = [
            pltpu.make_async_copy(
                ref, cache_ref.at[pl.ds(pl.multiple_of(at * half, 16), half), :], sem.at[slot]
            )
            for slot, (ref, at) in enumerate(zip(halves, (core, 1 - core)))
        ]
        for copy in copies:
            copy.start()
        for copy in copies:
            copy.wait()


def attend_kernel(kinds, rows, takes, caches, limit_at, latent, fresh_info, *refs):
    refs = list(refs)
    info_ref = refs.pop(0)
    cache_refs, refs = refs[:caches], refs[caches:]
    queries, rest = refs[: len(takes)], refs[len(takes) :]
    fresh_ref = rest.pop(0) if fresh_info else None
    fresh_rows = rest.pop() if fresh_info else None
    if caches > 1:
        sem, cache_ref = rest.pop(), rest.pop(-3)
        fetch_rows(info_ref, cache_refs[:2], cache_refs[2:], cache_ref, sem)
    else:
        cache_ref = cache_refs[0]
    score_ref, query_ref = rest.pop(-2), rest.pop()
    limit = info_ref[limit_at]
    sections = sections_of(rows)
    at = 0
    for ref, (start, stop) in zip(queries, takes):
        query_ref[at : at + stop - start, :] = ref[start:stop, :]
        at += stop - start
    peaks, totals, blocks = attend_block(query_ref[...], cache_ref, limit, score_ref, latent)
    for at, kind in enumerate(kinds):
        mine = slice(at * rows, (at + 1) * rows)
        peak, total, part = peaks[mine], totals[mine], blocks[mine]
        if kind == "own":
            query = query_ref[mine, :]
            other = fresh_block(query, fresh_ref, fresh_rows, *fresh_info, latent)
            top = jnp.maximum(peak, other[0])
            one, two = jnp.exp(peak - top), jnp.exp(other[0] - top)
            total = total * one + other[1] * two
            part = part * one + other[2] * two
            peak = top
        size = rows // sections
        cut = [slice(i * size, (i + 1) * size) for i in range(sections)]
        pieces = [(part[c], to_row(peak[c]), to_row(total[c])) for c in cut]
        if kind == "ends":
            for piece in pieces:
                store_packed(rest.pop(0), [piece])
            continue
        rest.pop(0)[...] = part
        stats_ref = rest.pop(0)
        line = lax.broadcasted_iota(jnp.int32, stats_ref.shape, 0)
        stats = jnp.zeros(stats_ref.shape, jnp.float32)
        for index, piece in enumerate(pieces):
            stats = jnp.where(line == 2 * index, piece[1], stats)
            stats = jnp.where(line == 2 * index + 1, piece[2], stats)
        stats_ref[...] = stats


def whole(memory=pltpu.VMEM):
    return pl.BlockSpec(memory_space=memory)


def attend(kinds, pieces, cache_parts, info, limit_at, latent, fresh=None, fresh_info=None):
    out_shape = []
    queries = [piece[0] for piece in pieces]
    takes = tuple(piece[1:] for piece in pieces)
    key_width = queries[0].shape[1]
    total = sum(stop - start for start, stop in takes)
    rows = total // len(kinds)
    sections = sections_of(rows)
    length = cache_parts[0].shape[1]
    flops = 2 * total * length * (key_width + latent)
    for kind in kinds:
        if kind == "ends":
            shape = (rows // sections + EXTRA, latent)
            out_shape += [jax.ShapeDtypeStruct(shape, jnp.bfloat16)] * sections
        else:
            out_shape.append(jax.ShapeDtypeStruct((rows, latent), jnp.float32))
            out_shape.append(jax.ShapeDtypeStruct((8, rows // sections), jnp.float32))
    operands = [info, *cache_parts, *queries] + ([fresh] if fresh_info else [])
    caches = len(cache_parts)
    scratch = [
        pltpu.VMEM((total, length), jnp.float32),
        pltpu.VMEM((total, key_width), jnp.bfloat16),
    ]
    if caches > 1:
        out_shape.append(jax.ShapeDtypeStruct((key_width, length), jnp.bfloat16))
        scratch.append(pltpu.SemaphoreType.DMA((2,)))
    if fresh_info:
        scratch.append(pltpu.VMEM((fresh.shape[0] * fresh.shape[1], key_width), jnp.float32))
    outs = pl.pallas_call(
        functools.partial(
            attend_kernel, tuple(kinds), rows, takes, caches, limit_at, latent, fresh_info
        ),
        out_shape=out_shape,
        in_specs=[whole(pltpu.SMEM)]
        + [whole(pl.ANY if caches > 1 else pltpu.VMEM)] * caches
        + [whole()] * (len(operands) - 1 - caches),
        out_specs=[whole()] * len(out_shape),
        scratch_shapes=scratch,
        compiler_params=pltpu.CompilerParams(vmem_limit_bytes=20 * MIB),
        cost_estimate=pl.CostEstimate(
            flops=flops, bytes_accessed=4 * MIB, transcendentals=total * length
        ),
        name="attend_" + "_".join(kinds),
    )(*operands)
    outs = list(outs)
    results = []
    for kind in kinds:
        size = sections if kind == "ends" else 2
        results.append(tuple(outs[:size]))
        outs = outs[size:]
    return results + outs


def merge_kernel(covers, *refs):
    refs = list(refs)
    outs = refs[len(refs) - len(covers) :]
    for cover, out_ref in zip(covers, outs):
        packed_ref = refs.pop(0) if cover else None
        part_ref, stats_ref = refs.pop(0), refs.pop(0)
        rows = stats_ref.shape[1]
        merged = []
        for at in range(part_ref.shape[0] // rows):
            piece = load_kept(part_ref, stats_ref, at)
            if at in cover:
                piece = combine(load_packed(packed_ref, rows, cover.index(at)), piece)
            merged.append(piece)
        store_packed(out_ref, merged)


def merge(items):
    operands, out_shape = [], []
    for packed, cover, (part, stats) in items:
        operands += ([packed] if cover else []) + [part, stats]
        shape = (part.shape[0] + EXTRA, part.shape[1])
        out_shape.append(jax.ShapeDtypeStruct(shape, jnp.bfloat16))
    return pl.pallas_call(
        functools.partial(merge_kernel, tuple(cover for _, cover, _ in items)),
        grid=(1,),
        out_shape=out_shape,
        in_specs=[pl.BlockSpec(operand.shape, lambda i: (0, 0)) for operand in operands],
        out_specs=[pl.BlockSpec(shape.shape, lambda i: (0, 0)) for shape in out_shape],
        compiler_params=pltpu.CompilerParams(vmem_limit_bytes=12 * MIB),
        cost_estimate=pl.CostEstimate(flops=1 << 20, bytes_accessed=2 * MIB, transcendentals=1024),
        name="merge",
    )(*operands)


def finish_kernel(chunks, heads, tile, *refs):
    value_ref, weight_ref, out_ref, rows_ref, values_ref, tiles_ref, sem = refs[-7:]
    copies = [
        pltpu.make_async_copy(
            weight_ref.at[:, at * tile : (at + 1) * tile], tiles_ref.at[at], sem.at[at]
        )
        for at in range(tiles_ref.shape[0])
    ]
    for copy in copies:
        copy.start()
    lanes = rows_ref.shape[0]
    end = 0
    for index in range(chunks):
        left_ref, right_ref, part_ref, stats_ref = refs[4 * index : 4 * index + 4]
        rows = stats_ref.shape[1]
        for at in range(part_ref.shape[0] // rows):
            merged, _, total = combine(
                load_packed(left_ref, rows, at),
                load_packed(right_ref, rows, at),
                load_kept(part_ref, stats_ref, at),
            )
            merged = merged / to_column(total)
            for lane in range(lanes):
                rows_ref[lane, end : end + rows, :] = merged[:, lane * 128 : (lane + 1) * 128]
            end += rows
    width = value_ref.shape[2]
    for head in range(heads):
        picked = pl.ds(head, end // heads, stride=heads)
        attended = jnp.concatenate([rows_ref[lane, picked, :] for lane in range(lanes)], axis=1)
        values = jnp.dot(
            attended.astype(jnp.bfloat16), value_ref[head], preferred_element_type=jnp.float32
        )
        values_ref[:, head * width : (head + 1) * width] = values.astype(jnp.bfloat16)
    values = values_ref[...]
    for at, copy in enumerate(copies):
        copy.wait()
        share = jnp.dot(values, tiles_ref[at], preferred_element_type=jnp.float32)
        if len(out_ref.shape) == 3:
            out_ref[at] = share.astype(out_ref.dtype)
        else:
            out_ref[:, at * tile : (at + 1) * tile] = share.astype(out_ref.dtype)


def finish(chunk_parts, value_up, out_proj, parts):
    heads, latent, width = value_up.shape
    depth, columns = out_proj.shape
    operands = []
    rows = 0
    for left, right, (part, stats) in chunk_parts:
        operands += [left, right, part, stats]
        rows += part.shape[0]
    lines = rows // heads
    share = columns // parts
    if share % 128 == 0:
        tile, shape = share, (parts, lines, share)
    else:
        tile, shape = columns // 8 if columns % 1024 == 0 else columns, (lines, columns)
    out = pl.pallas_call(
        functools.partial(finish_kernel, len(chunk_parts), heads, tile),
        out_shape=jax.ShapeDtypeStruct(shape, jnp.bfloat16),
        in_specs=[whole()] * (len(operands) + 1) + [whole(pltpu.HBM)],
        out_specs=whole(),
        scratch_shapes=[
            pltpu.VMEM((latent // 128, rows, 128), jnp.float32),
            pltpu.VMEM((lines, depth), jnp.bfloat16),
            pltpu.VMEM((columns // tile, depth, tile), jnp.bfloat16),
            pltpu.SemaphoreType.DMA((columns // tile,)),
        ],
        compiler_params=pltpu.CompilerParams(vmem_limit_bytes=44 * MIB),
        cost_estimate=pl.CostEstimate(
            flops=2 * lines * depth * columns,
            bytes_accessed=2 * depth * columns,
            transcendentals=1024,
        ),
        name="finish",
    )(*operands, value_up, out_proj)
    if share % 128:
        out = out.reshape(lines, parts, share).transpose(1, 0, 2)
    return out


def plan_kernel(group_ref, place_ref, lengths_ref, donor_ref, info_ref, *, local_len, half):
    group, place = group_ref[0], place_ref[0]
    source = donor_ref[group]
    first = place * local_len
    info_ref[0] = jnp.clip(lengths_ref[group] - first, 0, local_len)
    info_ref[1] = jnp.clip(lengths_ref[source] - first, 0, local_len)
    info_ref[2] = group
    info_ref[3] = source
    core, plane = group & 1, group >> 1
    wanted, crowded = [], []
    for at in range(2):
        one, two = donor_ref[2 * at], donor_ref[2 * at + 1]
        one_far, two_far = (one >> 1) != at, (two >> 1) != at
        wanted.append(jnp.where(one_far, one, two))
        crowded.append(one_far & two_far & (one != two))
    asked = jnp.where(plane == 0, wanted[1], wanted[0])
    info_ref[4] = jnp.where((asked & 1) == core, 1, 0)
    info_ref[5] = core * half
    info_ref[6] = jnp.where(crowded[0] | crowded[1], 1, 0)
    info_ref[7] = (1 - core) * half


def plan(lengths, donor, local_len, half):
    return pl.pallas_call(
        functools.partial(plan_kernel, local_len=local_len, half=half),
        out_shape=jax.ShapeDtypeStruct((8,), jnp.int32),
        in_specs=[whole(pltpu.SMEM)] * 4,
        out_specs=whole(pltpu.SMEM),
        name="plan",
    )(
        lax.axis_index("grp").reshape(1),
        lax.axis_index("ctx").reshape(1),
        lengths,
        donor,
    )


def offer_kernel(info_ref, own_ref, beside_ref, out_ref, sem):
    half = out_ref.shape[0]
    start = pl.multiple_of((info_ref[2] & 1) * half, 16)

    @pl.when(info_ref[4] == 1)
    def _():
        copy = pltpu.make_async_copy(own_ref.at[pl.ds(start, half), :], out_ref, sem)
        copy.start()
        copy.wait()

    @pl.when(info_ref[4] != 1)
    def _():
        copy = pltpu.make_async_copy(beside_ref.at[pl.ds(start, half), :], out_ref, sem)
        copy.start()
        copy.wait()


def offer(info, own, beside):
    half = own.shape[0] // 2
    return pl.pallas_call(
        offer_kernel,
        out_shape=jax.ShapeDtypeStruct((half, own.shape[1]), own.dtype),
        in_specs=[whole(pltpu.SMEM), whole(pl.ANY), whole(pl.ANY)],
        out_specs=whole(),
        scratch_shapes=[pltpu.SemaphoreType.DMA],
        cost_estimate=pl.CostEstimate(flops=0, bytes_accessed=2 * MIB, transcendentals=0),
        name="offer",
    )(info, own, beside)


core_swap = functools.partial(lax.ppermute, axis_name="grp", perm=[(g, g ^ 1) for g in range(4)])
plane_swap = functools.partial(lax.ppermute, axis_name="grp", perm=[(g, g ^ 2) for g in range(4)])


def exchange_all(cache_t, info):
    half = cache_t.shape[0] // 2
    across = plane_swap(cache_t)
    corner = core_swap(across)
    rows = jnp.where(info[3] == info[2] ^ 2, across, corner)
    return (
        lax.dynamic_slice_in_dim(rows, info[5], half, 0),
        lax.dynamic_slice_in_dim(rows, info[7], half, 0),
    )


def tie(came, other):
    values, other = lax.optimization_barrier(([value for value, _ in came], other))
    return [(value, cover) for value, (_, cover) in zip(values, came)], other


def body(cache, queries, new_latent, lengths, donor, value_up, out_proj):
    parts = lax.axis_size("ctx")
    steps, _, samples, heads, key_width = queries.shape
    latent = value_up.shape[1]
    cache_t = jnp.swapaxes(cache[0], 0, 1)
    local_len = cache_t.shape[1]
    info = plan(lengths, donor, local_len, key_width // 2)
    fresh = new_latent.reshape(steps, samples, key_width)

    ring = list(range(0, parts, 2)) + list(range(parts - 1, 0, -2))
    to_right = [(ring[i], ring[(i + 1) % parts]) for i in range(parts)]
    to_left = [(b, a) for a, b in to_right]
    right = functools.partial(lax.ppermute, axis_name="ctx", perm=to_right)
    left = functools.partial(lax.ppermute, axis_name="ctx", perm=to_left)
    reach = parts // 2

    step_rows = samples * heads
    mine_rows = queries.reshape(steps * step_rows, key_width)
    rows, cut = steps * step_rows, HANDOVER * step_rows
    half = rows // 2 if rows % 32 == 0 else rows
    four = lax.axis_size("grp") == 4
    if four:
        beside = core_swap(cache_t)

    lefts, rights = [mine_rows], [mine_rows]

    def pieces_of(hop, start, stop):
        if hop == 0:
            return [(mine_rows, start, stop)]
        if hop < reach:
            return [(lefts[hop], start, stop), (rights[hop], start, stop)]
        found = []
        for block, first in ((lefts[hop], 0), (rights[hop], half)):
            low, high = max(start, first), min(stop, first + half)
            if low < high and block is not None:
                found.append((block, low - first, high - first))
        return found

    def attend_early(hop):
        pieces = pieces_of(hop, 0, cut)
        if hop == 0:
            return attend(["own"], pieces, [cache_t], info, 0, latent, fresh, (0, heads))
        kinds = ["ends"] if hop == reach else ["keep", "keep"]
        return attend(kinds, pieces, [cache_t], info, 0, latent)

    early_parts = []
    for hop in range(1, reach + 1):
        if hop < reach:
            came = (right(lefts[-1]), left(rights[-1]))
        else:
            came = (
                right(lefts[-1][:half]),
                left(rights[-1][half:]) if half < rows else None,
            )
        extra = offer(info, cache_t, beside) if hop == 1 and four else None
        came, extra, parts_now = lax.optimization_barrier((came, extra, attend_early(hop - 1)))
        if hop == 1 and four:
            far_half = plane_swap(extra)
        lefts.append(came[0])
        rights.append(came[1])
        early_parts.append(parts_now)
    early_parts.append(attend_early(reach))

    if four:
        far_half, lefts[reach] = lax.optimization_barrier((far_half, lefts[reach]))
        far_rest = core_swap(far_half)
        far_half, far_rest = lax.cond(
            info[6] != 0, exchange_all, lambda *_: (far_half, far_rest), cache_t, info
        )
        moved = [cache_t, beside, far_half, far_rest]
    else:
        shards = lax.all_gather(cache_t, "grp", axis=0, tiled=False)
        found = lax.dynamic_index_in_dim(shards, info[3], 0, keepdims=False)
        moved = [found, found, found[: key_width // 2], found[key_width // 2 :]]
    *late_ends, moved_rows = attend(["ends"], pieces_of(reach, cut, rows), moved, info, 1, latent)

    def start_back(ends):
        ends = ends[0]
        sections = tuple(range(len(ends)))
        return [(ends[0], (0,)), (ends[1], (1,)) if len(ends) > 1 else (None, ())], sections

    def hop_back(going):
        (to_the_left, cover_left), (to_the_right, cover_right) = going
        return [
            (left(to_the_left), cover_left),
            (right(to_the_right) if cover_right else None, cover_right),
        ]

    def merge_back(came, kept, sections):
        merged = merge([(*item, block) for item, block in zip(came, kept)])
        return [(block, sections) for block in merged]

    early_going, sections = start_back(early_parts[reach])
    early_came = hop_back(early_going)
    early_came, late_ends = tie(early_came, late_ends)
    late_going, late_sections = start_back(late_ends)
    kinds, pieces = ["own"], pieces_of(0, cut, rows)
    for hop in range(1, reach):
        kinds += ["keep", "keep"]
        pieces += pieces_of(hop, cut, rows)
    results = attend(kinds, pieces, [moved_rows], info, 1, latent, fresh, (HANDOVER, heads))
    late_came = hop_back(late_going)
    for hop in range(reach - 1, 0, -1):
        early_came = hop_back(merge_back(early_came, early_parts[hop], sections))
        if hop == reach - 1:
            values = [value for value, _ in late_came]
            early_came, (results, values) = tie(early_came, (results, values))
            late_came = [(value, cover) for value, (_, cover) in zip(values, late_came)]
    late_parts = [[results[0]]]
    for hop in range(1, reach):
        late_parts.append(results[2 * hop - 1 : 2 * hop + 1])
    for hop in range(reach - 1, 0, -1):
        late_came = hop_back(merge_back(late_came, late_parts[hop], late_sections))
    finals = [
        (came[0][0], came[1][0], own[0])
        for came, own in ((early_came, early_parts[0]), (late_came, late_parts[0]))
    ]

    term = finish(finals, value_up, out_proj, parts)
    shares = lax.all_to_all(term, "ctx", split_axis=0, concat_axis=0, tiled=True)
    mixed = jnp.sum(shares.astype(jnp.float32), axis=0).astype(jnp.bfloat16)
    return mixed.reshape(steps, 1, samples, mixed.shape[-1])


def solution(mesh):
    return jax.shard_map(
        body,
        mesh=mesh,
        in_specs=(
            P("grp", "ctx", None),
            P(None, "grp", None, "ctx", None),
            P(None, "grp", None, None),
            P(),
            P(),
            P("ctx", None, None),
            P("ctx", None),
        ),
        out_specs=P(None, "grp", None, "ctx"),
        check_vma=False,
    )
```

```python
import functools

import jax
import jax.numpy as jnp
from jax import lax
from jax.experimental import pallas as pl
from jax.experimental.pallas import tpu as pltpu
from jax.sharding import PartitionSpec as P

HANDOVER = 3
EXTRA = 16
MIB = 1 << 20

score_scale = 192.0 ** (-0.5)
far_below = -1e30

ROWS_BY_ROWS = (((1,), (1,)), ((), ()))


def diagonal(n):
    return lax.broadcasted_iota(jnp.int32, (n, n), 0) == lax.broadcasted_iota(jnp.int32, (n, n), 1)


def to_row(column):
    n = column.shape[0]
    return jnp.sum(jnp.where(diagonal(n), column, 0.0), axis=0, keepdims=True)


def to_column(row):
    n = row.shape[1]
    return jnp.sum(jnp.where(diagonal(n), row, 0.0), axis=1, keepdims=True)


def split_three(value):
    high = value.astype(jnp.bfloat16).astype(jnp.float32)
    rest = value - high
    middle = rest.astype(jnp.bfloat16).astype(jnp.float32)
    return high, middle, rest - middle


def sections_of(rows):
    return 2 if rows % 32 == 0 else 1


def store_packed(out_ref, sections):
    rows, width = sections[0][0].shape
    end = rows * len(sections)
    line = lax.broadcasted_iota(jnp.int32, (EXTRA, rows), 0)
    block = jnp.zeros((EXTRA, rows), jnp.float32)
    for at, (part, peak, total) in enumerate(sections):
        out_ref[at * rows : (at + 1) * rows, :] = part.astype(jnp.bfloat16)
        for index, piece in enumerate(split_three(peak) + split_three(total)):
            block = jnp.where(line == 6 * at + index, piece, block)
    if rows < width:
        out_ref[end : end + EXTRA, :] = jnp.zeros((EXTRA, width), jnp.bfloat16)
    out_ref[end : end + EXTRA, 0:rows] = block.astype(jnp.bfloat16)


def load_packed(ref, rows, at):
    end = ref.shape[0] - EXTRA
    block = ref[end : end + EXTRA, 0:rows].astype(jnp.float32)
    line = [block[6 * at + i : 6 * at + i + 1] for i in range(6)]
    part = ref[at * rows : (at + 1) * rows, :].astype(jnp.float32)
    return part, line[0] + line[1] + line[2], line[3] + line[4] + line[5]


def load_kept(part_ref, stats_ref, at):
    rows = stats_ref.shape[1]
    part = part_ref[at * rows : (at + 1) * rows, :]
    return part, stats_ref[2 * at : 2 * at + 1, :], stats_ref[2 * at + 1 : 2 * at + 2, :]


def combine(*parts):
    peak = functools.reduce(jnp.maximum, [part[1] for part in parts])
    factors = [jnp.exp(part[1] - peak) for part in parts]
    total = sum(part[2] * factor for part, factor in zip(parts, factors))
    merged = sum(part[0] * to_column(factor) for part, factor in zip(parts, factors))
    return merged, peak, total


def attend_block(query, cache_ref, limit, score_ref, latent):
    rows = query.shape[0]
    length = cache_ref.shape[1]
    tile = min(512, length)
    peak = jnp.full((rows, 1), far_below, jnp.float32)
    for start in range(0, length, tile):
        scores = (
            jnp.dot(
                query, cache_ref[:, start : start + tile], preferred_element_type=jnp.float32
            )
            * score_scale
        )
        position = start + lax.broadcasted_iota(jnp.int32, (1, tile), 1)
        scores = jnp.where(position < limit, scores, far_below)
        score_ref[0:rows, start : start + tile] = scores
        peak = jnp.maximum(peak, jnp.max(scores, axis=1, keepdims=True))
    total = jnp.zeros((rows, 1), jnp.float32)
    part = jnp.zeros((rows, latent), jnp.float32)
    for start in range(0, length, tile):
        weights = jnp.exp(score_ref[0:rows, start : start + tile] - peak)
        total = total + jnp.sum(weights, axis=1, keepdims=True)
        part = part + lax.dot_general(
            weights.astype(jnp.bfloat16),
            cache_ref[0:latent, start : start + tile],
            ROWS_BY_ROWS,
            preferred_element_type=jnp.float32,
        )
    some = limit > 0
    return peak, jnp.where(some, total, 0.0), jnp.where(some, part, 0.0)


def fresh_block(query, fresh_ref, rows_ref, first_step, heads, latent):
    steps, samples, _ = fresh_ref.shape
    for step in range(steps):
        rows_ref[step * samples : (step + 1) * samples, :] = fresh_ref[step].astype(jnp.float32)
    fresh = rows_ref[...].astype(jnp.bfloat16)
    rows, columns = query.shape[0], fresh.shape[0]
    scores = (
        lax.dot_general(query, fresh, ROWS_BY_ROWS, preferred_element_type=jnp.float32)
        * score_scale
    )
    row = lax.broadcasted_iota(jnp.int32, (rows, columns), 0) // heads
    column = lax.broadcasted_iota(jnp.int32, (rows, columns), 1)
    seen = (column % samples == row % samples) & (column // samples <= row // samples + first_step)
    scores = jnp.where(seen, scores, far_below)
    peak = jnp.max(scores, axis=1, keepdims=True)
    weights = jnp.where(seen, jnp.exp(scores - peak), 0.0)
    total = jnp.sum(weights, axis=1, keepdims=True)
    part = jnp.dot(
        weights,
        rows_ref[:, 0:latent],
        precision=lax.Precision.HIGHEST,
        preferred_element_type=jnp.float32,
    )
    return peak, total, part


def fetch_rows(info_ref, sources, cache_ref, sem):
    own_ref, beside_ref, half_ref, rest_ref, spare_ref = sources
    me, source, crowded = info_ref[2], info_ref[3], info_ref[5] != 0
    half = half_ref.shape[0]
    near = (source >> 1) == (me >> 1)

    def whole_copy(ref):
        copy = pltpu.make_async_copy(ref, cache_ref, sem.at[0])
        copy.start()
        copy.wait()

    @pl.when(source == me)
    def _():
        whole_copy(own_ref)

    @pl.when(near & (source != me))
    def _():
        whole_copy(beside_ref)

    @pl.when(jnp.logical_not(near) & crowded)
    def _():
        whole_copy(spare_ref)

    @pl.when(jnp.logical_not(near | crowded))
    def _():
        core = me & 1
        copies = [
            pltpu.make_async_copy(
                ref, cache_ref.at[pl.ds(pl.multiple_of(at * half, 16), half), :], sem.at[slot]
            )
            for slot, (ref, at) in enumerate(((half_ref, core), (rest_ref, 1 - core)))
        ]
        for copy in copies:
            copy.start()
        for copy in copies:
            copy.wait()


def attend_kernel(kinds, rows, takes, caches, limit_at, latent, fresh_info, load, *refs):
    refs = list(refs)
    if load:
        load_sem, loaded_ref, weight_ref = refs.pop(), refs.pop(load[0]), refs.pop(load[1])
        loading = pltpu.make_async_copy(
            weight_ref.at[:, load[2] : load[3]], loaded_ref, load_sem
        )
        loading.start()
    info_ref = refs.pop(0)
    cache_refs, refs = refs[:caches], refs[caches:]
    queries, rest = refs[: len(takes)], refs[len(takes) :]
    fresh_ref = rest.pop(0) if fresh_info else None
    fresh_rows = rest.pop() if fresh_info else None
    if caches > 1:
        sem, cache_ref = rest.pop(), rest.pop(-3)
        fetch_rows(info_ref, cache_refs, cache_ref, sem)
    else:
        cache_ref = cache_refs[0]
    score_ref, query_ref = rest.pop(-2), rest.pop()
    limit = info_ref[limit_at]
    sections = sections_of(rows)
    at = 0
    for ref, (start, stop) in zip(queries, takes):
        query_ref[at : at + stop - start, :] = ref[start:stop, :]
        at += stop - start
    peaks, totals, blocks = attend_block(query_ref[...], cache_ref, limit, score_ref, latent)
    for at, kind in enumerate(kinds):
        mine = slice(at * rows, (at + 1) * rows)
        peak, total, part = peaks[mine], totals[mine], blocks[mine]
        if kind == "own":
            query = query_ref[mine, :]
            other = fresh_block(query, fresh_ref, fresh_rows, *fresh_info, latent)
            top = jnp.maximum(peak, other[0])
            one, two = jnp.exp(peak - top), jnp.exp(other[0] - top)
            total = total * one + other[1] * two
            part = part * one + other[2] * two
            peak = top
        size = rows // sections
        cut = [slice(i * size, (i + 1) * size) for i in range(sections)]
        pieces = [(part[c], to_row(peak[c]), to_row(total[c])) for c in cut]
        if kind == "ends":
            for piece in pieces:
                store_packed(rest.pop(0), [piece])
            continue
        rest.pop(0)[...] = part
        stats_ref = rest.pop(0)
        line = lax.broadcasted_iota(jnp.int32, stats_ref.shape, 0)
        stats = jnp.zeros(stats_ref.shape, jnp.float32)
        for index, piece in enumerate(pieces):
            stats = jnp.where(line == 2 * index, piece[1], stats)
            stats = jnp.where(line == 2 * index + 1, piece[2], stats)
        stats_ref[...] = stats
    if load:
        loading.wait()


def whole(memory=pltpu.VMEM):
    return pl.BlockSpec(memory_space=memory)


def in_hbm(array):
    return pltpu.with_memory_space_constraint(array, pltpu.HBM)


def attend(
    kinds, pieces, cache_parts, info, limit_at, latent, fresh=None, fresh_info=None, load=None
):
    out_shape = []
    queries = [piece[0] for piece in pieces]
    takes = tuple(piece[1:] for piece in pieces)
    key_width = queries[0].shape[1]
    total = sum(stop - start for start, stop in takes)
    rows = total // len(kinds)
    sections = sections_of(rows)
    length = cache_parts[0].shape[1]
    flops = 2 * total * length * (key_width + latent)
    for kind in kinds:
        if kind == "ends":
            shape = (rows // sections + EXTRA, latent)
            out_shape += [jax.ShapeDtypeStruct(shape, jnp.bfloat16)] * sections
        else:
            out_shape.append(jax.ShapeDtypeStruct((rows, latent), jnp.float32))
            out_shape.append(jax.ShapeDtypeStruct((8, rows // sections), jnp.float32))
    caches = len(cache_parts)
    if caches > 1:
        cache_parts = [in_hbm(part) for part in cache_parts]
    operands = [info, *cache_parts, *queries] + ([fresh] if fresh_info else [])
    scratch = [
        pltpu.VMEM((total, length), jnp.float32),
        pltpu.VMEM((total, key_width), jnp.bfloat16),
    ]
    if caches > 1:
        out_shape.append(jax.ShapeDtypeStruct((key_width, length), jnp.bfloat16))
        scratch.append(pltpu.SemaphoreType.DMA((2,)))
    if fresh_info:
        scratch.append(pltpu.VMEM((fresh.shape[0] * fresh.shape[1], key_width), jnp.float32))
    in_specs = (
        [whole(pltpu.SMEM)]
        + [whole(pltpu.HBM if caches > 1 else pltpu.VMEM)] * caches
        + [whole()] * (len(operands) - 1 - caches)
    )
    out_specs = [whole()] * len(out_shape)
    span = None
    if load:
        weight, start, stop = load
        operands.append(in_hbm(weight))
        in_specs.append(whole(pltpu.HBM))
        out_shape.append(pltpu.VMEM((weight.shape[0], stop - start), weight.dtype))
        out_specs.append(whole())
        scratch.append(pltpu.SemaphoreType.DMA)
        span = (len(operands) + len(out_shape) - 1, len(operands) - 1, start, stop)
    outs = pl.pallas_call(
        functools.partial(
            attend_kernel, tuple(kinds), rows, takes, caches, limit_at, latent, fresh_info, span
        ),
        out_shape=out_shape,
        in_specs=in_specs,
        out_specs=out_specs,
        scratch_shapes=scratch,
        compiler_params=pltpu.CompilerParams(vmem_limit_bytes=14 * MIB),
        cost_estimate=pl.CostEstimate(
            flops=flops, bytes_accessed=4 * MIB, transcendentals=total * length
        ),
        name="attend_" + "_".join(kinds),
    )(*operands)
    outs = list(outs)
    results = []
    for kind in kinds:
        size = sections if kind == "ends" else 2
        results.append(tuple(outs[:size]))
        outs = outs[size:]
    return results + outs


def merge_kernel(covers, *refs):
    refs = list(refs)
    outs = refs[len(refs) - len(covers) :]
    for cover, out_ref in zip(covers, outs):
        packed_ref = refs.pop(0) if cover else None
        part_ref, stats_ref = refs.pop(0), refs.pop(0)
        rows = stats_ref.shape[1]
        merged = []
        for at in range(part_ref.shape[0] // rows):
            piece = load_kept(part_ref, stats_ref, at)
            if at in cover:
                piece = combine(load_packed(packed_ref, rows, cover.index(at)), piece)
            merged.append(piece)
        store_packed(out_ref, merged)


def merge(items):
    operands, out_shape = [], []
    for packed, cover, (part, stats) in items:
        operands += ([packed] if cover else []) + [part, stats]
        shape = (part.shape[0] + EXTRA, part.shape[1])
        out_shape.append(jax.ShapeDtypeStruct(shape, jnp.bfloat16))
    return pl.pallas_call(
        functools.partial(merge_kernel, tuple(cover for _, cover, _ in items)),
        grid=(1,),
        out_shape=out_shape,
        in_specs=[pl.BlockSpec(operand.shape, lambda i: (0, 0)) for operand in operands],
        out_specs=[pl.BlockSpec(shape.shape, lambda i: (0, 0)) for shape in out_shape],
        compiler_params=pltpu.CompilerParams(vmem_limit_bytes=12 * MIB),
        cost_estimate=pl.CostEstimate(flops=1 << 20, bytes_accessed=2 * MIB, transcendentals=1024),
        name="merge",
    )(*operands)


def finish_kernel(chunks, heads, tile, *refs):
    value_ref = refs[4 * chunks]
    weight_refs = refs[4 * chunks + 1 : -3]
    out_ref, rows_ref, values_ref = refs[-3:]
    lanes = rows_ref.shape[0]
    end = 0
    for index in range(chunks):
        left_ref, right_ref, part_ref, stats_ref = refs[4 * index : 4 * index + 4]
        rows = stats_ref.shape[1]
        for at in range(part_ref.shape[0] // rows):
            merged, _, total = combine(
                load_packed(left_ref, rows, at),
                load_packed(right_ref, rows, at),
                load_kept(part_ref, stats_ref, at),
            )
            merged = merged / to_column(total)
            for lane in range(lanes):
                rows_ref[lane, end : end + rows, :] = merged[:, lane * 128 : (lane + 1) * 128]
            end += rows
    width = value_ref.shape[2]
    for head in range(heads):
        picked = pl.ds(head, end // heads, stride=heads)
        attended = jnp.concatenate([rows_ref[lane, picked, :] for lane in range(lanes)], axis=1)
        values = jnp.dot(
            attended.astype(jnp.bfloat16), value_ref[head], preferred_element_type=jnp.float32
        )
        values_ref[:, head * width : (head + 1) * width] = values.astype(jnp.bfloat16)
    values = values_ref[...]
    at = 0
    for weight_ref in weight_refs:
        for start in range(0, weight_ref.shape[1], tile):
            share = jnp.dot(
                values, weight_ref[:, start : start + tile], preferred_element_type=jnp.float32
            )
            if len(out_ref.shape) == 3:
                out_ref[at] = share.astype(out_ref.dtype)
            else:
                out_ref[:, at * tile : (at + 1) * tile] = share.astype(out_ref.dtype)
            at += 1


def finish(chunk_parts, value_up, weights, parts):
    heads, latent, width = value_up.shape
    depth = weights[0].shape[0]
    columns = sum(weight.shape[1] for weight in weights)
    operands = []
    rows = 0
    for left, right, (part, stats) in chunk_parts:
        operands += [left, right, part, stats]
        rows += part.shape[0]
    lines = rows // heads
    share = columns // parts
    if share % 128 == 0:
        tile, shape = share, (parts, lines, share)
    else:
        tile, shape = columns // 8, (lines, columns)
    out = pl.pallas_call(
        functools.partial(finish_kernel, len(chunk_parts), heads, tile),
        out_shape=jax.ShapeDtypeStruct(shape, jnp.bfloat16),
        in_specs=[whole()] * (len(operands) + 1 + len(weights)),
        out_specs=whole(),
        scratch_shapes=[
            pltpu.VMEM((latent // 128, rows, 128), jnp.float32),
            pltpu.VMEM((lines, depth), jnp.bfloat16),
        ],
        compiler_params=pltpu.CompilerParams(vmem_limit_bytes=10 * MIB),
        cost_estimate=pl.CostEstimate(
            flops=2 * lines * depth * columns,
            bytes_accessed=2 * depth * columns,
            transcendentals=1024,
        ),
        name="finish",
    )(*operands, value_up, *weights)
    if share % 128:
        out = out.reshape(lines, parts, share).transpose(1, 0, 2)
    return out


def plan_kernel(group_ref, place_ref, lengths_ref, donor_ref, info_ref, flag_ref, *, local_len):
    group, place = group_ref[0], place_ref[0]
    source = donor_ref[group]
    first = place * local_len
    info_ref[0] = jnp.clip(lengths_ref[group] - first, 0, local_len)
    info_ref[1] = jnp.clip(lengths_ref[source] - first, 0, local_len)
    info_ref[2] = group
    info_ref[3] = source
    core, plane = group & 1, group >> 1
    wanted, crowded = [], []
    for at in range(2):
        one, two = donor_ref[2 * at], donor_ref[2 * at + 1]
        one_far, two_far = (one >> 1) != at, (two >> 1) != at
        wanted.append(jnp.where(one_far, one, two))
        crowded.append(one_far & two_far & (one != two))
    asked = jnp.where(plane == 0, wanted[1], wanted[0])
    info_ref[4] = jnp.where((asked & 1) == core, 1, 0)
    flag = jnp.where(crowded[0] | crowded[1], 1, 0)
    info_ref[5] = flag
    flag_ref[0] = flag


def plan(lengths, donor, local_len):
    return pl.pallas_call(
        functools.partial(plan_kernel, local_len=local_len),
        out_shape=[jax.ShapeDtypeStruct((6,), jnp.int32), jax.ShapeDtypeStruct((1,), jnp.int32)],
        in_specs=[whole(pltpu.SMEM)] * 4,
        out_specs=[whole(pltpu.SMEM)] * 2,
        compiler_params=pltpu.CompilerParams(vmem_limit_bytes=MIB),
        name="plan",
    )(
        lax.axis_index("grp").reshape(1),
        lax.axis_index("ctx").reshape(1),
        lengths,
        donor,
    )


def offer_kernel(info_ref, own_ref, beside_ref, out_ref, sem):
    half = out_ref.shape[0]
    start = pl.multiple_of((info_ref[2] & 1) * half, 16)

    @pl.when(info_ref[4] == 1)
    def _():
        copy = pltpu.make_async_copy(own_ref.at[pl.ds(start, half), :], out_ref, sem)
        copy.start()
        copy.wait()

    @pl.when(info_ref[4] != 1)
    def _():
        copy = pltpu.make_async_copy(beside_ref.at[pl.ds(start, half), :], out_ref, sem)
        copy.start()
        copy.wait()


def offer(info, own, beside):
    half = own.shape[0] // 2
    return pl.pallas_call(
        offer_kernel,
        out_shape=pltpu.VMEM((half, own.shape[1]), own.dtype),
        in_specs=[whole(pltpu.SMEM), whole(pltpu.HBM), whole(pltpu.HBM)],
        out_specs=whole(),
        scratch_shapes=[pltpu.SemaphoreType.DMA],
        compiler_params=pltpu.CompilerParams(vmem_limit_bytes=4 * MIB),
        cost_estimate=pl.CostEstimate(flops=0, bytes_accessed=2 * MIB, transcendentals=0),
        name="offer",
    )(info, in_hbm(own), in_hbm(beside))


core_swap = functools.partial(lax.ppermute, axis_name="grp", perm=[(g, g ^ 1) for g in range(4)])
plane_swap = functools.partial(lax.ppermute, axis_name="grp", perm=[(g, g ^ 2) for g in range(4)])


def exchange_all(cache_t, info):
    across = plane_swap(cache_t)
    corner = core_swap(across)
    return jnp.where(info[3] == info[2] ^ 2, across, corner)


def blank(like):
    return pl.pallas_call(
        lambda out_ref: None,
        out_shape=jax.ShapeDtypeStruct(like.shape, like.dtype),
        out_specs=whole(pl.ANY),
        compiler_params=pltpu.CompilerParams(vmem_limit_bytes=MIB),
        name="blank",
    )()


def tie(came, other):
    values, other = lax.optimization_barrier(([value for value, _ in came], other))
    return [(value, cover) for value, (_, cover) in zip(values, came)], other


def body(cache, queries, new_latent, lengths, donor, value_up, out_proj):
    parts = lax.axis_size("ctx")
    steps, _, samples, heads, key_width = queries.shape
    latent = value_up.shape[1]
    cache_t = jnp.swapaxes(cache[0], 0, 1)
    local_len = cache_t.shape[1]
    info, crowded = plan(lengths, donor, local_len)
    fresh = new_latent.reshape(steps, samples, key_width)

    ring = list(range(0, parts, 2)) + list(range(parts - 1, 0, -2))
    to_right = [(ring[i], ring[(i + 1) % parts]) for i in range(parts)]
    to_left = [(b, a) for a, b in to_right]
    right = functools.partial(lax.ppermute, axis_name="ctx", perm=to_right)
    left = functools.partial(lax.ppermute, axis_name="ctx", perm=to_left)
    reach = parts // 2

    step_rows = samples * heads
    mine_rows = queries.reshape(steps * step_rows, key_width)
    rows, cut = steps * step_rows, HANDOVER * step_rows
    half = rows // 2 if rows % 32 == 0 else rows
    four = lax.axis_size("grp") == 4
    if four:
        beside = core_swap(cache_t)

    lefts, rights = [mine_rows], [mine_rows]

    def pieces_of(hop, start, stop):
        if hop == 0:
            return [(mine_rows, start, stop)]
        if hop < reach:
            return [(lefts[hop], start, stop), (rights[hop], start, stop)]
        found = []
        for block, first in ((lefts[hop], 0), (rights[hop], half)):
            low, high = max(start, first), min(stop, first + half)
            if low < high and block is not None:
                found.append((block, low - first, high - first))
        return found

    width = out_proj.shape[1]
    quarter = width // 4 if width % 512 == 0 else width
    loaded = []

    def attend_early(hop):
        pieces = pieces_of(hop, 0, cut)
        if hop == 0:
            return None
        kinds = ["ends"] if hop == reach else ["keep", "keep"]
        start = (hop - 1) * quarter
        if hop == reach or start >= width or hop > 2:
            return attend(kinds, pieces, [cache_t], info, 0, latent)
        load = (out_proj, start, start + quarter)
        *results, piece = attend(kinds, pieces, [cache_t], info, 0, latent, load=load)
        loaded.append(piece)
        return results

    early_parts = []
    for hop in range(1, reach + 1):
        if hop < reach:
            came = (right(lefts[-1]), left(rights[-1]))
        else:
            came = (
                right(lefts[-1][:half]),
                left(rights[-1][half:]) if half < rows else None,
            )
        extra = None
        if hop == 1 and four:
            extra = offer(info, cache_t, beside)
        elif hop == 2 and four:
            extra = lax.cond(
                crowded.reshape(()) != 0, exchange_all, lambda rows, _: blank(rows), cache_t, info
            )
        came, extra, parts_now = lax.optimization_barrier((came, extra, attend_early(hop - 1)))
        if hop == 1 and four:
            far_half = plane_swap(extra)
        elif hop == 2 and four:
            spare = extra
        lefts.append(came[0])
        rights.append(came[1])
        early_parts.append(parts_now)
    early_parts.append(attend_early(reach))

    if four:
        far_half, lefts[reach] = lax.optimization_barrier((far_half, lefts[reach]))
        moved = [cache_t, beside, far_half, core_swap(far_half), spare]
    else:
        shards = lax.all_gather(cache_t, "grp", axis=0, tiled=False)
        found = lax.dynamic_index_in_dim(shards, info[3], 0, keepdims=False)
        moved = [found, found, found[: key_width // 2], found[key_width // 2 :], found]
    *late_ends, moved_rows = attend(["ends"], pieces_of(reach, cut, rows), moved, info, 1, latent)

    def start_back(ends):
        ends = ends[0]
        sections = tuple(range(len(ends)))
        return [(ends[0], (0,)), (ends[1], (1,)) if len(ends) > 1 else (None, ())], sections

    def hop_back(going):
        (to_the_left, cover_left), (to_the_right, cover_right) = going
        return [
            (left(to_the_left), cover_left),
            (right(to_the_right) if cover_right else None, cover_right),
        ]

    def merge_back(came, kept, sections):
        merged = merge([(*item, block) for item, block in zip(came, kept)])
        return [(block, sections) for block in merged]

    early_going, sections = start_back(early_parts[reach])
    early_came = hop_back(early_going)
    early_came, late_ends = tie(early_came, late_ends)
    late_going, late_sections = start_back(late_ends)
    kinds, pieces = ["own"], pieces_of(0, cut, rows)
    for hop in range(1, reach):
        kinds += ["keep", "keep"]
        pieces += pieces_of(hop, cut, rows)

    def load_more(limit):
        start = quarter * len(loaded)
        stop = min(start + quarter, width) if limit else width
        return (out_proj, start, stop) if start < width else None

    load = load_more(True)
    results = attend(
        kinds, pieces, [moved_rows], info, 1, latent, fresh, (HANDOVER, heads), load
    )
    if load:
        loaded.append(results.pop())
    load = load_more(False)
    early_parts[0] = attend(
        ["own"], pieces_of(0, 0, cut), [cache_t], info, 0, latent, fresh, (0, heads), load
    )
    if load:
        loaded.append(early_parts[0].pop())
    late_came = hop_back(late_going)
    for hop in range(reach - 1, 0, -1):
        early_came = hop_back(merge_back(early_came, early_parts[hop], sections))
        if hop == reach - 1:
            values = [value for value, _ in late_came]
            early_came, (results, values) = tie(early_came, (results, values))
            late_came = [(value, cover) for value, (_, cover) in zip(values, late_came)]
    late_parts = [[results[0]]]
    for hop in range(1, reach):
        late_parts.append(results[2 * hop - 1 : 2 * hop + 1])
    for hop in range(reach - 1, 0, -1):
        late_came = hop_back(merge_back(late_came, late_parts[hop], late_sections))
    finals = [
        (came[0][0], came[1][0], own[0])
        for came, own in ((early_came, early_parts[0]), (late_came, late_parts[0]))
    ]

    term = finish(finals, value_up, loaded, parts)
    shares = lax.all_to_all(term, "ctx", split_axis=0, concat_axis=0, tiled=True)
    mixed = jnp.sum(shares.astype(jnp.float32), axis=0).astype(jnp.bfloat16)
    return mixed.reshape(steps, 1, samples, mixed.shape[-1])


def solution(mesh):
    return jax.shard_map(
        body,
        mesh=mesh,
        in_specs=(
            P("grp", "ctx", None),
            P(None, "grp", None, "ctx", None),
            P(None, "grp", None, None),
            P(),
            P(),
            P("ctx", None, None),
            P("ctx", None),
        ),
        out_specs=P(None, "grp", None, "ctx"),
        check_vma=False,
    )
```

```python
import functools

import jax
import jax.numpy as jnp
from jax import lax
from jax.experimental import pallas as pl
from jax.experimental.pallas import tpu as pltpu
from jax.sharding import PartitionSpec as P

HANDOVER = 3
EXTRA = 16
MIB = 1 << 20

score_scale = 192.0 ** (-0.5)
far_below = -1e30

ROWS_BY_ROWS = (((1,), (1,)), ((), ()))


def diagonal(n):
    return lax.broadcasted_iota(jnp.int32, (n, n), 0) == lax.broadcasted_iota(jnp.int32, (n, n), 1)


def to_row(column):
    n = column.shape[0]
    return jnp.sum(jnp.where(diagonal(n), column, 0.0), axis=0, keepdims=True)


def to_column(row):
    n = row.shape[1]
    return jnp.sum(jnp.where(diagonal(n), row, 0.0), axis=1, keepdims=True)


def split_three(value):
    high = value.astype(jnp.bfloat16).astype(jnp.float32)
    rest = value - high
    middle = rest.astype(jnp.bfloat16).astype(jnp.float32)
    return high, middle, rest - middle


def sections_of(rows):
    return 2 if rows % 32 == 0 else 1


def store_packed(out_ref, sections):
    rows, width = sections[0][0].shape
    end = rows * len(sections)
    line = lax.broadcasted_iota(jnp.int32, (EXTRA, rows), 0)
    block = jnp.zeros((EXTRA, rows), jnp.float32)
    for at, (part, peak, total) in enumerate(sections):
        out_ref[at * rows : (at + 1) * rows, :] = part.astype(jnp.bfloat16)
        for index, piece in enumerate(split_three(peak) + split_three(total)):
            block = jnp.where(line == 6 * at + index, piece, block)
    if rows < width:
        out_ref[end : end + EXTRA, :] = jnp.zeros((EXTRA, width), jnp.bfloat16)
    out_ref[end : end + EXTRA, 0:rows] = block.astype(jnp.bfloat16)


def load_packed(ref, rows, at):
    end = ref.shape[0] - EXTRA
    block = ref[end : end + EXTRA, 0:rows].astype(jnp.float32)
    line = [block[6 * at + i : 6 * at + i + 1] for i in range(6)]
    part = ref[at * rows : (at + 1) * rows, :].astype(jnp.float32)
    return part, line[0] + line[1] + line[2], line[3] + line[4] + line[5]


def load_kept(part_ref, stats_ref, at):
    rows = stats_ref.shape[1]
    part = part_ref[at * rows : (at + 1) * rows, :]
    return part, stats_ref[2 * at : 2 * at + 1, :], stats_ref[2 * at + 1 : 2 * at + 2, :]


def combine(*parts):
    peak = functools.reduce(jnp.maximum, [part[1] for part in parts])
    factors = [jnp.exp(part[1] - peak) for part in parts]
    total = sum(part[2] * factor for part, factor in zip(parts, factors))
    merged = sum(part[0] * to_column(factor) for part, factor in zip(parts, factors))
    return merged, peak, total


def attend_block(query, cache_ref, limit, score_ref, latent):
    rows = query.shape[0]
    length = cache_ref.shape[1]
    tile = min(512, length)
    peak = jnp.full((rows, 1), far_below, jnp.float32)
    for start in range(0, length, tile):
        scores = (
            jnp.dot(
                query, cache_ref[:, start : start + tile], preferred_element_type=jnp.float32
            )
            * score_scale
        )
        position = start + lax.broadcasted_iota(jnp.int32, (1, tile), 1)
        scores = jnp.where(position < limit, scores, far_below)
        score_ref[0:rows, start : start + tile] = scores
        peak = jnp.maximum(peak, jnp.max(scores, axis=1, keepdims=True))
    total = jnp.zeros((rows, 1), jnp.float32)
    part = jnp.zeros((rows, latent), jnp.float32)
    for start in range(0, length, tile):
        weights = jnp.exp(score_ref[0:rows, start : start + tile] - peak)
        total = total + jnp.sum(weights, axis=1, keepdims=True)
        part = part + lax.dot_general(
            weights.astype(jnp.bfloat16),
            cache_ref[0:latent, start : start + tile],
            ROWS_BY_ROWS,
            preferred_element_type=jnp.float32,
        )
    some = limit > 0
    return peak, jnp.where(some, total, 0.0), jnp.where(some, part, 0.0)


def fresh_block(query, fresh_ref, rows_ref, first_step, heads, latent):
    steps, samples, _ = fresh_ref.shape
    for step in range(steps):
        rows_ref[step * samples : (step + 1) * samples, :] = fresh_ref[step].astype(jnp.float32)
    fresh = rows_ref[...].astype(jnp.bfloat16)
    rows, columns = query.shape[0], fresh.shape[0]
    scores = (
        lax.dot_general(query, fresh, ROWS_BY_ROWS, preferred_element_type=jnp.float32)
        * score_scale
    )
    row = lax.broadcasted_iota(jnp.int32, (rows, columns), 0) // heads
    column = lax.broadcasted_iota(jnp.int32, (rows, columns), 1)
    seen = (column % samples == row % samples) & (column // samples <= row // samples + first_step)
    scores = jnp.where(seen, scores, far_below)
    peak = jnp.max(scores, axis=1, keepdims=True)
    weights = jnp.where(seen, jnp.exp(scores - peak), 0.0)
    total = jnp.sum(weights, axis=1, keepdims=True)
    part = jnp.dot(
        weights,
        rows_ref[:, 0:latent],
        precision=lax.Precision.HIGHEST,
        preferred_element_type=jnp.float32,
    )
    return peak, total, part


def fetch_rows(info_ref, sources, cache_ref, sem):
    own_ref, beside_ref, half_ref, rest_ref, spare_ref = sources
    me, source, crowded = info_ref[2], info_ref[3], info_ref[5] != 0
    half = half_ref.shape[0]
    near = (source >> 1) == (me >> 1)

    def whole_copy(ref):
        copy = pltpu.make_async_copy(ref, cache_ref, sem.at[0])
        copy.start()
        copy.wait()

    @pl.when(source == me)
    def _():
        whole_copy(own_ref)

    @pl.when(near & (source != me))
    def _():
        whole_copy(beside_ref)

    @pl.when(jnp.logical_not(near) & crowded)
    def _():
        whole_copy(spare_ref)

    @pl.when(jnp.logical_not(near | crowded))
    def _():
        core = me & 1
        copies = [
            pltpu.make_async_copy(
                ref, cache_ref.at[pl.ds(pl.multiple_of(at * half, 16), half), :], sem.at[slot]
            )
            for slot, (ref, at) in enumerate(((half_ref, core), (rest_ref, 1 - core)))
        ]
        for copy in copies:
            copy.start()
        for copy in copies:
            copy.wait()


def attend_kernel(kinds, rows, takes, caches, limit_at, latent, fresh_info, load, *refs):
    refs = list(refs)
    if load:
        load_sem, loaded_ref, weight_ref = refs.pop(), refs.pop(load[0]), refs.pop(load[1])
        loading = pltpu.make_async_copy(
            weight_ref.at[:, load[2] : load[3]], loaded_ref, load_sem
        )
        loading.start()
    info_ref = refs.pop(0)
    cache_refs, refs = refs[:caches], refs[caches:]
    queries, rest = refs[: len(takes)], refs[len(takes) :]
    fresh_ref = rest.pop(0) if fresh_info else None
    fresh_rows = rest.pop() if fresh_info else None
    if caches > 1:
        sem, cache_ref = rest.pop(), rest.pop(-3)
        fetch_rows(info_ref, cache_refs, cache_ref, sem)
    else:
        cache_ref = cache_refs[0]
    score_ref, query_ref = rest.pop(-2), rest.pop()
    limit = info_ref[limit_at]
    sections = sections_of(rows)
    at = 0
    for ref, (start, stop) in zip(queries, takes):
        query_ref[at : at + stop - start, :] = ref[start:stop, :]
        at += stop - start
    peaks, totals, blocks = attend_block(query_ref[...], cache_ref, limit, score_ref, latent)
    for at, kind in enumerate(kinds):
        mine = slice(at * rows, (at + 1) * rows)
        peak, total, part = peaks[mine], totals[mine], blocks[mine]
        if kind == "own":
            query = query_ref[mine, :]
            other = fresh_block(query, fresh_ref, fresh_rows, *fresh_info, latent)
            top = jnp.maximum(peak, other[0])
            one, two = jnp.exp(peak - top), jnp.exp(other[0] - top)
            total = total * one + other[1] * two
            part = part * one + other[2] * two
            peak = top
        size = rows // sections
        cut = [slice(i * size, (i + 1) * size) for i in range(sections)]
        pieces = [(part[c], to_row(peak[c]), to_row(total[c])) for c in cut]
        if kind == "ends":
            for piece in pieces:
                store_packed(rest.pop(0), [piece])
            continue
        rest.pop(0)[...] = part
        stats_ref = rest.pop(0)
        line = lax.broadcasted_iota(jnp.int32, stats_ref.shape, 0)
        stats = jnp.zeros(stats_ref.shape, jnp.float32)
        for index, piece in enumerate(pieces):
            stats = jnp.where(line == 2 * index, piece[1], stats)
            stats = jnp.where(line == 2 * index + 1, piece[2], stats)
        stats_ref[...] = stats
    if load:
        loading.wait()


def whole(memory=pltpu.VMEM):
    return pl.BlockSpec(memory_space=memory)


def in_hbm(array):
    return pltpu.with_memory_space_constraint(array, pltpu.HBM)


def attend(
    kinds, pieces, cache_parts, info, limit_at, latent, fresh=None, fresh_info=None, load=None
):
    out_shape = []
    queries = [piece[0] for piece in pieces]
    takes = tuple(piece[1:] for piece in pieces)
    key_width = queries[0].shape[1]
    total = sum(stop - start for start, stop in takes)
    rows = total // len(kinds)
    sections = sections_of(rows)
    length = cache_parts[0].shape[1]
    flops = 2 * total * length * (key_width + latent)
    for kind in kinds:
        if kind == "ends":
            shape = (rows // sections + EXTRA, latent)
            out_shape += [jax.ShapeDtypeStruct(shape, jnp.bfloat16)] * sections
        else:
            out_shape.append(jax.ShapeDtypeStruct((rows, latent), jnp.float32))
            out_shape.append(jax.ShapeDtypeStruct((8, rows // sections), jnp.float32))
    caches = len(cache_parts)
    if caches > 1:
        cache_parts = [
            part if part.shape[0] < key_width else in_hbm(part) for part in cache_parts
        ]
    operands = [info, *cache_parts, *queries] + ([fresh] if fresh_info else [])
    scratch = [
        pltpu.VMEM((total, length), jnp.float32),
        pltpu.VMEM((total, key_width), jnp.bfloat16),
    ]
    if caches > 1:
        out_shape.append(jax.ShapeDtypeStruct((key_width, length), jnp.bfloat16))
        scratch.append(pltpu.SemaphoreType.DMA((2,)))
    if fresh_info:
        scratch.append(pltpu.VMEM((fresh.shape[0] * fresh.shape[1], key_width), jnp.float32))
    in_specs = (
        [whole(pltpu.SMEM)]
        + [whole(pl.ANY if caches > 1 else pltpu.VMEM)] * caches
        + [whole()] * (len(operands) - 1 - caches)
    )
    out_specs = [whole()] * len(out_shape)
    span = None
    if load:
        weight, start, stop = load
        operands.append(in_hbm(weight))
        in_specs.append(whole(pltpu.HBM))
        out_shape.append(pltpu.VMEM((weight.shape[0], stop - start), weight.dtype))
        out_specs.append(whole())
        scratch.append(pltpu.SemaphoreType.DMA)
        span = (len(operands) + len(out_shape) - 1, len(operands) - 1, start, stop)
    outs = pl.pallas_call(
        functools.partial(
            attend_kernel, tuple(kinds), rows, takes, caches, limit_at, latent, fresh_info, span
        ),
        out_shape=out_shape,
        in_specs=in_specs,
        out_specs=out_specs,
        scratch_shapes=scratch,
        compiler_params=pltpu.CompilerParams(vmem_limit_bytes=14 * MIB),
        cost_estimate=pl.CostEstimate(
            flops=flops, bytes_accessed=4 * MIB, transcendentals=total * length
        ),
        name="attend_" + "_".join(kinds),
    )(*operands)
    outs = list(outs)
    results = []
    for kind in kinds:
        size = sections if kind == "ends" else 2
        results.append(tuple(outs[:size]))
        outs = outs[size:]
    return results + outs


def load_kernel(start, stop, weight_ref, out_ref, sem):
    copy = pltpu.make_async_copy(weight_ref.at[:, start:stop], out_ref, sem)
    copy.start()
    copy.wait()


def load_alone(weight, start, stop):
    return pl.pallas_call(
        functools.partial(load_kernel, start, stop),
        out_shape=pltpu.VMEM((weight.shape[0], stop - start), weight.dtype),
        in_specs=[whole(pltpu.HBM)],
        out_specs=whole(),
        scratch_shapes=[pltpu.SemaphoreType.DMA],
        compiler_params=pltpu.CompilerParams(vmem_limit_bytes=MIB),
        cost_estimate=pl.CostEstimate(
            flops=0, bytes_accessed=2 * weight.shape[0] * (stop - start), transcendentals=0
        ),
        name="load",
    )(in_hbm(weight))


def merge_kernel(covers, *refs):
    refs = list(refs)
    outs = refs[len(refs) - len(covers) :]
    for item, out_ref in zip(covers, outs):
        packed_refs = [refs.pop(0) for _ in item]
        part_ref, stats_ref = refs.pop(0), refs.pop(0)
        rows = stats_ref.shape[1]
        merged = []
        for at in range(part_ref.shape[0] // rows):
            pieces = [
                load_packed(packed_ref, rows, cover.index(at))
                for packed_ref, cover in zip(packed_refs, item)
                if at in cover
            ]
            kept = load_kept(part_ref, stats_ref, at)
            merged.append(combine(*pieces, kept) if pieces else kept)
        store_packed(out_ref, merged)


def merge(items):
    operands, out_shape = [], []
    for packed, (part, stats) in items:
        operands += [block for block, _ in packed] + [part, stats]
        shape = (part.shape[0] + EXTRA, part.shape[1])
        out_shape.append(jax.ShapeDtypeStruct(shape, jnp.bfloat16))
    covers = tuple(tuple(cover for _, cover in packed) for packed, _ in items)
    return pl.pallas_call(
        functools.partial(merge_kernel, covers),
        grid=(1,),
        out_shape=out_shape,
        in_specs=[pl.BlockSpec(operand.shape, lambda i: (0, 0)) for operand in operands],
        out_specs=[pl.BlockSpec(shape.shape, lambda i: (0, 0)) for shape in out_shape],
        compiler_params=pltpu.CompilerParams(vmem_limit_bytes=12 * MIB),
        cost_estimate=pl.CostEstimate(flops=1 << 20, bytes_accessed=2 * MIB, transcendentals=1024),
        name="merge",
    )(*operands)


def finish_kernel(chunks, heads, tile, *refs):
    value_ref = refs[4 * chunks]
    weight_refs = refs[4 * chunks + 1 : -3]
    out_ref, rows_ref, values_ref = refs[-3:]
    lanes = rows_ref.shape[0]
    end = 0
    for index in range(chunks):
        left_ref, right_ref, part_ref, stats_ref = refs[4 * index : 4 * index + 4]
        rows = stats_ref.shape[1]
        for at in range(part_ref.shape[0] // rows):
            merged, _, total = combine(
                load_packed(left_ref, rows, at),
                load_packed(right_ref, rows, at),
                load_kept(part_ref, stats_ref, at),
            )
            merged = merged / to_column(total)
            for lane in range(lanes):
                rows_ref[lane, end : end + rows, :] = merged[:, lane * 128 : (lane + 1) * 128]
            end += rows
    width = value_ref.shape[2]
    for head in range(heads):
        picked = pl.ds(head, end // heads, stride=heads)
        attended = jnp.concatenate([rows_ref[lane, picked, :] for lane in range(lanes)], axis=1)
        values = jnp.dot(
            attended.astype(jnp.bfloat16), value_ref[head], preferred_element_type=jnp.float32
        )
        values_ref[:, head * width : (head + 1) * width] = values.astype(jnp.bfloat16)
    values = values_ref[...]
    at = 0
    for weight_ref in weight_refs:
        for start in range(0, weight_ref.shape[1], tile):
            share = jnp.dot(
                values, weight_ref[:, start : start + tile], preferred_element_type=jnp.float32
            )
            if len(out_ref.shape) == 3:
                out_ref[at] = share.astype(out_ref.dtype)
            else:
                out_ref[:, at * tile : (at + 1) * tile] = share.astype(out_ref.dtype)
            at += 1


def finish(chunk_parts, value_up, weights, parts):
    heads, latent, width = value_up.shape
    depth = weights[0].shape[0]
    columns = sum(weight.shape[1] for weight in weights)
    operands = []
    rows = 0
    for left, right, (part, stats) in chunk_parts:
        operands += [left, right, part, stats]
        rows += part.shape[0]
    lines = rows // heads
    share = columns // parts
    if share % 128 == 0:
        tile, shape = share, (parts, lines, share)
    else:
        tile, shape = columns // 8 if columns % 1024 == 0 else columns, (lines, columns)
    out = pl.pallas_call(
        functools.partial(finish_kernel, len(chunk_parts), heads, tile),
        out_shape=jax.ShapeDtypeStruct(shape, jnp.bfloat16),
        in_specs=[whole()] * (len(operands) + 1 + len(weights)),
        out_specs=whole(),
        scratch_shapes=[
            pltpu.VMEM((latent // 128, rows, 128), jnp.float32),
            pltpu.VMEM((lines, depth), jnp.bfloat16),
        ],
        compiler_params=pltpu.CompilerParams(vmem_limit_bytes=10 * MIB),
        cost_estimate=pl.CostEstimate(
            flops=2 * lines * depth * columns,
            bytes_accessed=2 * depth * columns,
            transcendentals=1024,
        ),
        name="finish",
    )(*operands, value_up, *weights)
    if share % 128:
        out = out.reshape(lines, parts, share).transpose(1, 0, 2)
    return out


def plan_kernel(group_ref, place_ref, lengths_ref, donor_ref, info_ref, flag_ref, *, local_len):
    group, place = group_ref[0], place_ref[0]
    source = donor_ref[group]
    first = place * local_len
    info_ref[0] = jnp.clip(lengths_ref[group] - first, 0, local_len)
    info_ref[1] = jnp.clip(lengths_ref[source] - first, 0, local_len)
    info_ref[2] = group
    info_ref[3] = source
    core, plane = group & 1, group >> 1
    wanted, crowded = [], []
    for at in range(2):
        one, two = donor_ref[2 * at], donor_ref[2 * at + 1]
        one_far, two_far = (one >> 1) != at, (two >> 1) != at
        wanted.append(jnp.where(one_far, one, two))
        crowded.append(one_far & two_far & (one != two))
    asked = jnp.where(plane == 0, wanted[1], wanted[0])
    info_ref[4] = jnp.where((asked & 1) == core, 1, 0)
    flag = jnp.where(crowded[0] | crowded[1], 1, 0)
    info_ref[5] = flag
    flag_ref[0] = flag


def plan(lengths, donor, local_len):
    return pl.pallas_call(
        functools.partial(plan_kernel, local_len=local_len),
        out_shape=[jax.ShapeDtypeStruct((6,), jnp.int32), jax.ShapeDtypeStruct((1,), jnp.int32)],
        in_specs=[whole(pltpu.SMEM)] * 4,
        out_specs=[whole(pltpu.SMEM)] * 2,
        compiler_params=pltpu.CompilerParams(vmem_limit_bytes=MIB),
        name="plan",
    )(
        lax.axis_index("grp").reshape(1),
        lax.axis_index("ctx").reshape(1),
        lengths,
        donor,
    )


def offer_kernel(info_ref, own_ref, beside_ref, out_ref, sem):
    half = out_ref.shape[0]
    start = pl.multiple_of((info_ref[2] & 1) * half, 16)

    @pl.when(info_ref[4] == 1)
    def _():
        copy = pltpu.make_async_copy(own_ref.at[pl.ds(start, half), :], out_ref, sem)
        copy.start()
        copy.wait()

    @pl.when(info_ref[4] != 1)
    def _():
        copy = pltpu.make_async_copy(beside_ref.at[pl.ds(start, half), :], out_ref, sem)
        copy.start()
        copy.wait()


def offer(info, own, beside):
    half = own.shape[0] // 2
    return pl.pallas_call(
        offer_kernel,
        out_shape=pltpu.VMEM((half, own.shape[1]), own.dtype),
        in_specs=[whole(pltpu.SMEM), whole(pltpu.HBM), whole(pltpu.HBM)],
        out_specs=whole(),
        scratch_shapes=[pltpu.SemaphoreType.DMA],
        compiler_params=pltpu.CompilerParams(vmem_limit_bytes=4 * MIB),
        cost_estimate=pl.CostEstimate(flops=0, bytes_accessed=2 * MIB, transcendentals=0),
        name="offer",
    )(info, in_hbm(own), in_hbm(beside))


core_swap = functools.partial(lax.ppermute, axis_name="grp", perm=[(g, g ^ 1) for g in range(4)])
plane_swap = functools.partial(lax.ppermute, axis_name="grp", perm=[(g, g ^ 2) for g in range(4)])


def exchange_all(cache_t, info):
    across = plane_swap(cache_t)
    corner = core_swap(across)
    return jnp.where(info[3] == info[2] ^ 2, across, corner)


def tie(*trees):
    leaves, structure = jax.tree.flatten(trees)
    places = [at for at, leaf in enumerate(leaves) if isinstance(leaf, jax.Array)]
    held = lax.optimization_barrier([leaves[at] for at in places])
    for at, leaf in zip(places, held):
        leaves[at] = leaf
    return jax.tree.unflatten(structure, leaves)


def blank(like):
    return pl.pallas_call(
        lambda out_ref: None,
        out_shape=jax.ShapeDtypeStruct(like.shape, like.dtype),
        out_specs=whole(pl.ANY),
        compiler_params=pltpu.CompilerParams(vmem_limit_bytes=MIB),
        name="blank",
    )()


def body(cache, queries, new_latent, lengths, donor, value_up, out_proj):
    parts = lax.axis_size("ctx")
    steps, _, samples, heads, key_width = queries.shape
    latent = value_up.shape[1]
    cache_t = jnp.swapaxes(cache[0], 0, 1)
    local_len = cache_t.shape[1]
    info, crowded = plan(lengths, donor, local_len)
    fresh = new_latent.reshape(steps, samples, key_width)

    ring = list(range(0, parts, 2)) + list(range(parts - 1, 0, -2))
    to_right = [(ring[i], ring[(i + 1) % parts]) for i in range(parts)]
    to_left = [(b, a) for a, b in to_right]
    right = functools.partial(lax.ppermute, axis_name="ctx", perm=to_right)
    left = functools.partial(lax.ppermute, axis_name="ctx", perm=to_left)
    reach = parts // 2

    step_rows = samples * heads
    mine_rows = queries.reshape(steps * step_rows, key_width)
    rows, cut = steps * step_rows, HANDOVER * step_rows
    half = rows // 2 if rows % 32 == 0 else rows
    four = lax.axis_size("grp") == 4
    if four:
        beside = core_swap(cache_t)

    lefts, rights = [mine_rows], [mine_rows]

    def pieces_of(hop, start, stop):
        if hop == 0:
            return [(mine_rows, start, stop)]
        if hop < reach:
            return [(lefts[hop], start, stop), (rights[hop], start, stop)]
        found = []
        for block, first in ((lefts[hop], 0), (rights[hop], half)):
            low, high = max(start, first), min(stop, first + half)
            if low < high and block is not None:
                found.append((block, low - first, high - first))
        return found

    width = out_proj.shape[1]
    unit = width // 8 if width % 1024 == 0 else width
    loads = (2, 2)
    loaded = []

    def load_next(units):
        start = sum(piece.shape[1] for piece in loaded)
        stop = min(start + units * unit, width)
        return (out_proj, start, stop) if start < stop else None

    def attend_more(kinds, pieces, units, *rest):
        load = load_next(units)
        results = attend(kinds, pieces, [cache_t], info, 0, latent, *rest, load=load)
        if load:
            loaded.append(results.pop())
        return results

    def attend_early(hop):
        if hop == 0:
            return None
        kinds = ["ends"] if hop == reach else ["keep", "keep"]
        units = loads[hop - 1] if hop <= len(loads) else 0
        return attend_more(kinds, pieces_of(hop, 0, cut), units)

    early_parts = []
    for hop in range(1, reach + 1):
        if hop < reach:
            came = (right(lefts[-1]), left(rights[-1]))
        else:
            came = (
                right(lefts[-1][:half]),
                left(rights[-1][half:]) if half < rows else None,
            )
        extra = None
        if hop == 1 and four:
            extra = offer(info, cache_t, beside)
        elif hop == 2 and four:
            extra = lax.cond(
                crowded.reshape(()) != 0, exchange_all, lambda rows, _: blank(rows), cache_t, info
            )
        came, extra, parts_now = tie(came, extra, attend_early(hop - 1))
        if hop == 1 and four:
            far_half = plane_swap(extra)
        elif hop == 2 and four:
            spare = extra
        lefts.append(came[0])
        rights.append(came[1])
        early_parts.append(parts_now)
    early_parts.append(attend_early(reach))

    if four:
        far_half, lefts[reach] = tie(far_half, lefts[reach])
        moved = [cache_t, beside, far_half, core_swap(far_half), spare]
    else:
        shards = lax.all_gather(cache_t, "grp", axis=0, tiled=False)
        found = lax.dynamic_index_in_dim(shards, info[3], 0, keepdims=False)
        moved = [found, found, found[: key_width // 2], found[key_width // 2 :], found]
    near = reach - 1
    late_ends, *late_near, moved_rows = attend(
        ["ends", "keep", "keep"],
        pieces_of(reach, cut, rows) + pieces_of(near, cut, rows),
        moved,
        info,
        1,
        latent,
    )

    sections = tuple(range(sections_of(cut)))
    late_sections = tuple(range(sections_of(rows - cut)))

    def hop_back(going):
        return [
            [(send(block), cover) for block, cover in items]
            for send, items in zip((left, right), going)
        ]

    def merge_back(came, kept, sections):
        return [[(block, sections)] for block in merge(list(zip(came, kept)))]

    def ends_back(ends):
        return [[(ends[0], (0,))], [(ends[1], (1,))] if len(ends) > 1 else []]

    early_came = hop_back(ends_back(early_parts[reach][0]))
    early_came, late_ends, late_near = tie(early_came, late_ends, late_near)
    late_came = hop_back(ends_back(late_ends))
    early_came = hop_back(merge_back(early_came, early_parts[near], sections))
    kinds, pieces = ["own"], pieces_of(0, cut, rows)
    for hop in range(1, near):
        kinds += ["keep", "keep"]
        pieces += pieces_of(hop, cut, rows)
    results = attend(kinds, pieces, [moved_rows], info, 1, latent, fresh, (HANDOVER, heads))
    late_came, results = tie(late_came, results)
    late_came = hop_back(merge_back(late_came, late_near, late_sections))
    early_came, late_came = tie(early_came, late_came)

    early_parts[0] = attend_more(["own"], pieces_of(0, 0, cut), 0, fresh, (0, heads))
    late_parts = [[results[0]]]
    for hop in range(1, near):
        late_parts.append(results[2 * hop - 1 : 2 * hop + 1])
    for hop in range(near - 1, 0, -1):
        early_came = hop_back(merge_back(early_came, early_parts[hop], sections))
        late_came = hop_back(merge_back(late_came, late_parts[hop], late_sections))
        early_came, late_came, early_parts[0] = tie(early_came, late_came, early_parts[0])
    load = load_next(8)
    if load:
        loaded.append(load_alone(*load))
    finals = [
        (came[0][0][0], came[1][0][0], own[0])
        for came, own in ((early_came, early_parts[0]), (late_came, late_parts[0]))
    ]

    term = finish(finals, value_up, loaded, parts)
    shares = lax.all_to_all(term, "ctx", split_axis=0, concat_axis=0, tiled=True)
    mixed = jnp.sum(shares.astype(jnp.float32), axis=0).astype(jnp.bfloat16)
    return mixed.reshape(steps, 1, samples, mixed.shape[-1])


def solution(mesh):
    return jax.shard_map(
        body,
        mesh=mesh,
        in_specs=(
            P("grp", "ctx", None),
            P(None, "grp", None, "ctx", None),
            P(None, "grp", None, None),
            P(),
            P(),
            P("ctx", None, None),
            P("ctx", None),
        ),
        out_specs=P(None, "grp", None, "ctx"),
        check_vma=False,
    )
```

```python
import functools

import jax
import jax.numpy as jnp
from jax import lax
from jax.experimental import pallas as pl
from jax.experimental.pallas import tpu as pltpu
from jax.sharding import PartitionSpec as P

HANDOVER = 3
EXTRA = 16
MIB = 1 << 20

score_scale = 192.0 ** (-0.5)
far_below = -1e30

ROWS_BY_ROWS = (((1,), (1,)), ((), ()))


def diagonal(n):
    return lax.broadcasted_iota(jnp.int32, (n, n), 0) == lax.broadcasted_iota(jnp.int32, (n, n), 1)


def to_row(column):
    n = column.shape[0]
    return jnp.sum(jnp.where(diagonal(n), column, 0.0), axis=0, keepdims=True)


def to_column(row):
    n = row.shape[1]
    return jnp.sum(jnp.where(diagonal(n), row, 0.0), axis=1, keepdims=True)


def split_three(value):
    high = value.astype(jnp.bfloat16).astype(jnp.float32)
    rest = value - high
    middle = rest.astype(jnp.bfloat16).astype(jnp.float32)
    return high, middle, rest - middle


def sections_of(rows):
    return 2 if rows % 32 == 0 else 1


def store_packed(out_ref, sections):
    rows, width = sections[0][0].shape
    end = rows * len(sections)
    line = lax.broadcasted_iota(jnp.int32, (EXTRA, rows), 0)
    block = jnp.zeros((EXTRA, rows), jnp.float32)
    for at, (part, peak, total) in enumerate(sections):
        out_ref[at * rows : (at + 1) * rows, :] = part.astype(jnp.bfloat16)
        for index, piece in enumerate(split_three(peak) + split_three(total)):
            block = jnp.where(line == 6 * at + index, piece, block)
    if rows < width:
        out_ref[end : end + EXTRA, :] = jnp.zeros((EXTRA, width), jnp.bfloat16)
    out_ref[end : end + EXTRA, 0:rows] = block.astype(jnp.bfloat16)


def load_packed(ref, rows, at):
    end = ref.shape[0] - EXTRA
    block = ref[end : end + EXTRA, 0:rows].astype(jnp.float32)
    line = [block[6 * at + i : 6 * at + i + 1] for i in range(6)]
    part = ref[at * rows : (at + 1) * rows, :].astype(jnp.float32)
    return part, line[0] + line[1] + line[2], line[3] + line[4] + line[5]


def load_kept(part_ref, stats_ref, at):
    rows = stats_ref.shape[1]
    part = part_ref[at * rows : (at + 1) * rows, :]
    return part, stats_ref[2 * at : 2 * at + 1, :], stats_ref[2 * at + 1 : 2 * at + 2, :]


def combine(*parts):
    peak = functools.reduce(jnp.maximum, [part[1] for part in parts])
    factors = [jnp.exp(part[1] - peak) for part in parts]
    total = sum(part[2] * factor for part, factor in zip(parts, factors))
    merged = sum(part[0] * to_column(factor) for part, factor in zip(parts, factors))
    return merged, peak, total


def attend_block(query, cache_ref, limit, score_ref, latent):
    rows = query.shape[0]
    length = cache_ref.shape[1]
    tile = min(512, length)
    peak = jnp.full((rows, 1), far_below, jnp.float32)
    for start in range(0, length, tile):
        scores = (
            jnp.dot(
                query, cache_ref[:, start : start + tile], preferred_element_type=jnp.float32
            )
            * score_scale
        )
        position = start + lax.broadcasted_iota(jnp.int32, (1, tile), 1)
        scores = jnp.where(position < limit, scores, far_below)
        score_ref[0:rows, start : start + tile] = scores
        peak = jnp.maximum(peak, jnp.max(scores, axis=1, keepdims=True))
    total = jnp.zeros((rows, 1), jnp.float32)
    part = jnp.zeros((rows, latent), jnp.float32)
    for start in range(0, length, tile):
        weights = jnp.exp(score_ref[0:rows, start : start + tile] - peak)
        total = total + jnp.sum(weights, axis=1, keepdims=True)
        part = part + lax.dot_general(
            weights.astype(jnp.bfloat16),
            cache_ref[0:latent, start : start + tile],
            ROWS_BY_ROWS,
            preferred_element_type=jnp.float32,
        )
    some = limit > 0
    return peak, jnp.where(some, total, 0.0), jnp.where(some, part, 0.0)


def fresh_block(query, fresh_ref, rows_ref, first_step, heads, latent):
    steps, samples, _ = fresh_ref.shape
    for step in range(steps):
        rows_ref[step * samples : (step + 1) * samples, :] = fresh_ref[step].astype(jnp.float32)
    fresh = rows_ref[...].astype(jnp.bfloat16)
    rows, columns = query.shape[0], fresh.shape[0]
    scores = (
        lax.dot_general(query, fresh, ROWS_BY_ROWS, preferred_element_type=jnp.float32)
        * score_scale
    )
    row = lax.broadcasted_iota(jnp.int32, (rows, columns), 0) // heads
    column = lax.broadcasted_iota(jnp.int32, (rows, columns), 1)
    seen = (column % samples == row % samples) & (column // samples <= row // samples + first_step)
    scores = jnp.where(seen, scores, far_below)
    peak = jnp.max(scores, axis=1, keepdims=True)
    weights = jnp.where(seen, jnp.exp(scores - peak), 0.0)
    total = jnp.sum(weights, axis=1, keepdims=True)
    part = jnp.dot(
        weights,
        rows_ref[:, 0:latent],
        precision=lax.Precision.HIGHEST,
        preferred_element_type=jnp.float32,
    )
    return peak, total, part


def fetch_rows(info_ref, sources, cache_ref, sem):
    own_ref, beside_ref, half_ref, rest_ref, spare_ref = sources
    me, source, crowded = info_ref[2], info_ref[3], info_ref[5] != 0
    half = half_ref.shape[0]
    near = (source >> 1) == (me >> 1)

    def whole_copy(ref):
        copy = pltpu.make_async_copy(ref, cache_ref, sem.at[0])
        copy.start()
        copy.wait()

    @pl.when(source == me)
    def _():
        whole_copy(own_ref)

    @pl.when(near & (source != me))
    def _():
        whole_copy(beside_ref)

    @pl.when(jnp.logical_not(near) & crowded)
    def _():
        whole_copy(spare_ref)

    @pl.when(jnp.logical_not(near | crowded))
    def _():
        core = me & 1
        copies = [
            pltpu.make_async_copy(
                ref, cache_ref.at[pl.ds(pl.multiple_of(at * half, 16), half), :], sem.at[slot]
            )
            for slot, (ref, at) in enumerate(((half_ref, core), (rest_ref, 1 - core)))
        ]
        for copy in copies:
            copy.start()
        for copy in copies:
            copy.wait()


def attend_kernel(kinds, rows, takes, caches, limit_at, latent, fresh_info, load, *refs):
    refs = list(refs)
    if load:
        load_sem, loaded_ref, weight_ref = refs.pop(), refs.pop(load[0]), refs.pop(load[1])
        loading = pltpu.make_async_copy(
            weight_ref.at[:, load[2] : load[3]], loaded_ref, load_sem
        )
        loading.start()
    info_ref = refs.pop(0)
    cache_refs, refs = refs[:caches], refs[caches:]
    queries, rest = refs[: len(takes)], refs[len(takes) :]
    fresh_ref = rest.pop(0) if fresh_info else None
    fresh_rows = rest.pop() if fresh_info else None
    if caches > 1:
        sem, cache_ref = rest.pop(), rest.pop(-3)
        fetch_rows(info_ref, cache_refs, cache_ref, sem)
    else:
        cache_ref = cache_refs[0]
    score_ref, query_ref = rest.pop(-2), rest.pop()
    limit = info_ref[limit_at]
    sections = sections_of(rows)
    at = 0
    for ref, (start, stop) in zip(queries, takes):
        query_ref[at : at + stop - start, :] = ref[start:stop, :]
        at += stop - start
    peaks, totals, blocks = attend_block(query_ref[...], cache_ref, limit, score_ref, latent)
    for at, kind in enumerate(kinds):
        mine = slice(at * rows, (at + 1) * rows)
        peak, total, part = peaks[mine], totals[mine], blocks[mine]
        if kind == "own":
            query = query_ref[mine, :]
            other = fresh_block(query, fresh_ref, fresh_rows, *fresh_info, latent)
            top = jnp.maximum(peak, other[0])
            one, two = jnp.exp(peak - top), jnp.exp(other[0] - top)
            total = total * one + other[1] * two
            part = part * one + other[2] * two
            peak = top
        size = rows // sections
        cut = [slice(i * size, (i + 1) * size) for i in range(sections)]
        pieces = [(part[c], to_row(peak[c]), to_row(total[c])) for c in cut]
        if kind == "ends":
            for piece in pieces:
                store_packed(rest.pop(0), [piece])
            continue
        rest.pop(0)[...] = part
        stats_ref = rest.pop(0)
        line = lax.broadcasted_iota(jnp.int32, stats_ref.shape, 0)
        stats = jnp.zeros(stats_ref.shape, jnp.float32)
        for index, piece in enumerate(pieces):
            stats = jnp.where(line == 2 * index, piece[1], stats)
            stats = jnp.where(line == 2 * index + 1, piece[2], stats)
        stats_ref[...] = stats
    if load:
        loading.wait()


def whole(memory=pltpu.VMEM):
    return pl.BlockSpec(memory_space=memory)


def in_hbm(array):
    return pltpu.with_memory_space_constraint(array, pltpu.HBM)


def attend(
    kinds, pieces, cache_parts, info, limit_at, latent, fresh=None, fresh_info=None, load=None
):
    out_shape = []
    queries = [piece[0] for piece in pieces]
    takes = tuple(piece[1:] for piece in pieces)
    key_width = queries[0].shape[1]
    total = sum(stop - start for start, stop in takes)
    rows = total // len(kinds)
    sections = sections_of(rows)
    length = cache_parts[0].shape[1]
    flops = 2 * total * length * (key_width + latent)
    for kind in kinds:
        if kind == "ends":
            shape = (rows // sections + EXTRA, latent)
            out_shape += [jax.ShapeDtypeStruct(shape, jnp.bfloat16)] * sections
        else:
            out_shape.append(jax.ShapeDtypeStruct((rows, latent), jnp.float32))
            out_shape.append(jax.ShapeDtypeStruct((8, rows // sections), jnp.float32))
    caches = len(cache_parts)
    if caches > 1:
        cache_parts = [
            part if part.shape[0] < key_width else in_hbm(part) for part in cache_parts
        ]
    operands = [info, *cache_parts, *queries] + ([fresh] if fresh_info else [])
    scratch = [
        pltpu.VMEM((total, length), jnp.float32),
        pltpu.VMEM((total, key_width), jnp.bfloat16),
    ]
    if caches > 1:
        out_shape.append(jax.ShapeDtypeStruct((key_width, length), jnp.bfloat16))
        scratch.append(pltpu.SemaphoreType.DMA((2,)))
    if fresh_info:
        scratch.append(pltpu.VMEM((fresh.shape[0] * fresh.shape[1], key_width), jnp.float32))
    in_specs = (
        [whole(pltpu.SMEM)]
        + [whole(pl.ANY if caches > 1 else pltpu.VMEM)] * caches
        + [whole()] * (len(operands) - 1 - caches)
    )
    out_specs = [whole()] * len(out_shape)
    span = None
    if load:
        weight, start, stop = load
        operands.append(in_hbm(weight))
        in_specs.append(whole(pltpu.HBM))
        out_shape.append(pltpu.VMEM((weight.shape[0], stop - start), weight.dtype))
        out_specs.append(whole())
        scratch.append(pltpu.SemaphoreType.DMA)
        span = (len(operands) + len(out_shape) - 1, len(operands) - 1, start, stop)
    outs = pl.pallas_call(
        functools.partial(
            attend_kernel, tuple(kinds), rows, takes, caches, limit_at, latent, fresh_info, span
        ),
        out_shape=out_shape,
        in_specs=in_specs,
        out_specs=out_specs,
        scratch_shapes=scratch,
        compiler_params=pltpu.CompilerParams(vmem_limit_bytes=14 * MIB),
        cost_estimate=pl.CostEstimate(
            flops=flops, bytes_accessed=4 * MIB, transcendentals=total * length
        ),
        name="attend_" + "_".join(kinds),
    )(*operands)
    outs = list(outs)
    results = []
    for kind in kinds:
        size = sections if kind == "ends" else 2
        results.append(tuple(outs[:size]))
        outs = outs[size:]
    return results + outs


def load_kernel(start, stop, weight_ref, out_ref, sem):
    copy = pltpu.make_async_copy(weight_ref.at[:, start:stop], out_ref, sem)
    copy.start()
    copy.wait()


def load_alone(weight, start, stop):
    return pl.pallas_call(
        functools.partial(load_kernel, start, stop),
        out_shape=pltpu.VMEM((weight.shape[0], stop - start), weight.dtype),
        in_specs=[whole(pltpu.HBM)],
        out_specs=whole(),
        scratch_shapes=[pltpu.SemaphoreType.DMA],
        compiler_params=pltpu.CompilerParams(vmem_limit_bytes=MIB),
        cost_estimate=pl.CostEstimate(
            flops=0, bytes_accessed=2 * weight.shape[0] * (stop - start), transcendentals=0
        ),
        name="load",
    )(in_hbm(weight))


def merge_kernel(covers, *refs):
    refs = list(refs)
    outs = refs[len(refs) - len(covers) :]
    for item, out_ref in zip(covers, outs):
        packed_refs = [refs.pop(0) for _ in item]
        part_ref, stats_ref = refs.pop(0), refs.pop(0)
        rows = stats_ref.shape[1]
        merged = []
        for at in range(part_ref.shape[0] // rows):
            pieces = [
                load_packed(packed_ref, rows, cover.index(at))
                for packed_ref, cover in zip(packed_refs, item)
                if at in cover
            ]
            kept = load_kept(part_ref, stats_ref, at)
            merged.append(combine(*pieces, kept) if pieces else kept)
        store_packed(out_ref, merged)


def merge(items):
    operands, out_shape = [], []
    for packed, (part, stats) in items:
        operands += [block for block, _ in packed] + [part, stats]
        shape = (part.shape[0] + EXTRA, part.shape[1])
        out_shape.append(jax.ShapeDtypeStruct(shape, jnp.bfloat16))
    covers = tuple(tuple(cover for _, cover in packed) for packed, _ in items)
    return pl.pallas_call(
        functools.partial(merge_kernel, covers),
        grid=(1,),
        out_shape=out_shape,
        in_specs=[pl.BlockSpec(operand.shape, lambda i: (0, 0)) for operand in operands],
        out_specs=[pl.BlockSpec(shape.shape, lambda i: (0, 0)) for shape in out_shape],
        compiler_params=pltpu.CompilerParams(vmem_limit_bytes=12 * MIB),
        cost_estimate=pl.CostEstimate(flops=1 << 20, bytes_accessed=2 * MIB, transcendentals=1024),
        name="merge",
    )(*operands)


def finish_kernel(chunks, heads, tile, *refs):
    value_ref = refs[4 * chunks]
    weight_refs = refs[4 * chunks + 1 : -3]
    out_ref, rows_ref, values_ref = refs[-3:]
    lanes = rows_ref.shape[0]
    end = 0
    for index in range(chunks):
        left_ref, right_ref, part_ref, stats_ref = refs[4 * index : 4 * index + 4]
        rows = stats_ref.shape[1]
        for at in range(part_ref.shape[0] // rows):
            merged, _, total = combine(
                load_packed(left_ref, rows, at),
                load_packed(right_ref, rows, at),
                load_kept(part_ref, stats_ref, at),
            )
            merged = merged / to_column(total)
            for lane in range(lanes):
                rows_ref[lane, end : end + rows, :] = merged[:, lane * 128 : (lane + 1) * 128]
            end += rows
    width = value_ref.shape[2]
    for head in range(heads):
        picked = pl.ds(head, end // heads, stride=heads)
        attended = jnp.concatenate([rows_ref[lane, picked, :] for lane in range(lanes)], axis=1)
        values = jnp.dot(
            attended.astype(jnp.bfloat16), value_ref[head], preferred_element_type=jnp.float32
        )
        values_ref[:, head * width : (head + 1) * width] = values.astype(jnp.bfloat16)
    values = values_ref[...]
    at = 0
    for weight_ref in weight_refs:
        for start in range(0, weight_ref.shape[1], tile):
            share = jnp.dot(
                values, weight_ref[:, start : start + tile], preferred_element_type=jnp.float32
            )
            if len(out_ref.shape) == 3:
                out_ref[at] = share.astype(out_ref.dtype)
            else:
                out_ref[:, at * tile : (at + 1) * tile] = share.astype(out_ref.dtype)
            at += 1


def finish(chunk_parts, value_up, weights, parts):
    heads, latent, width = value_up.shape
    depth = weights[0].shape[0]
    columns = sum(weight.shape[1] for weight in weights)
    operands = []
    rows = 0
    for left, right, (part, stats) in chunk_parts:
        operands += [left, right, part, stats]
        rows += part.shape[0]
    lines = rows // heads
    share = columns // parts
    if share % 128 == 0:
        tile, shape = share, (parts, lines, share)
    else:
        tile, shape = columns // 8 if columns % 1024 == 0 else columns, (lines, columns)
    out = pl.pallas_call(
        functools.partial(finish_kernel, len(chunk_parts), heads, tile),
        out_shape=jax.ShapeDtypeStruct(shape, jnp.bfloat16),
        in_specs=[whole()] * (len(operands) + 1 + len(weights)),
        out_specs=whole(),
        scratch_shapes=[
            pltpu.VMEM((latent // 128, rows, 128), jnp.float32),
            pltpu.VMEM((lines, depth), jnp.bfloat16),
        ],
        compiler_params=pltpu.CompilerParams(vmem_limit_bytes=10 * MIB),
        cost_estimate=pl.CostEstimate(
            flops=2 * lines * depth * columns,
            bytes_accessed=2 * depth * columns,
            transcendentals=1024,
        ),
        name="finish",
    )(*operands, value_up, *weights)
    if share % 128:
        out = out.reshape(lines, parts, share).transpose(1, 0, 2)
    return out


def plan_kernel(group_ref, place_ref, lengths_ref, donor_ref, info_ref, flag_ref, *, local_len):
    group, place = group_ref[0], place_ref[0]
    source = donor_ref[group]
    first = place * local_len
    info_ref[0] = jnp.clip(lengths_ref[group] - first, 0, local_len)
    info_ref[1] = jnp.clip(lengths_ref[source] - first, 0, local_len)
    info_ref[2] = group
    info_ref[3] = source
    core, plane = group & 1, group >> 1
    wanted, crowded = [], []
    for at in range(2):
        one, two = donor_ref[2 * at], donor_ref[2 * at + 1]
        one_far, two_far = (one >> 1) != at, (two >> 1) != at
        wanted.append(jnp.where(one_far, one, two))
        crowded.append(one_far & two_far & (one != two))
    asked = jnp.where(plane == 0, wanted[1], wanted[0])
    info_ref[4] = jnp.where((asked & 1) == core, 1, 0)
    flag = jnp.where(crowded[0] | crowded[1], 1, 0)
    info_ref[5] = flag
    flag_ref[0] = flag


def plan(lengths, donor, local_len):
    return pl.pallas_call(
        functools.partial(plan_kernel, local_len=local_len),
        out_shape=[jax.ShapeDtypeStruct((6,), jnp.int32), jax.ShapeDtypeStruct((1,), jnp.int32)],
        in_specs=[whole(pltpu.SMEM)] * 4,
        out_specs=[whole(pltpu.SMEM)] * 2,
        compiler_params=pltpu.CompilerParams(vmem_limit_bytes=MIB),
        name="plan",
    )(
        lax.axis_index("grp").reshape(1),
        lax.axis_index("ctx").reshape(1),
        lengths,
        donor,
    )


def offer_kernel(info_ref, own_ref, beside_ref, out_ref, sem):
    half = out_ref.shape[0]
    start = pl.multiple_of((info_ref[2] & 1) * half, 16)

    @pl.when(info_ref[4] == 1)
    def _():
        copy = pltpu.make_async_copy(own_ref.at[pl.ds(start, half), :], out_ref, sem)
        copy.start()
        copy.wait()

    @pl.when(info_ref[4] != 1)
    def _():
        copy = pltpu.make_async_copy(beside_ref.at[pl.ds(start, half), :], out_ref, sem)
        copy.start()
        copy.wait()


def offer(info, own, beside):
    half = own.shape[0] // 2
    return pl.pallas_call(
        offer_kernel,
        out_shape=pltpu.VMEM((half, own.shape[1]), own.dtype),
        in_specs=[whole(pltpu.SMEM), whole(pltpu.HBM), whole(pltpu.HBM)],
        out_specs=whole(),
        scratch_shapes=[pltpu.SemaphoreType.DMA],
        compiler_params=pltpu.CompilerParams(vmem_limit_bytes=4 * MIB),
        cost_estimate=pl.CostEstimate(flops=0, bytes_accessed=2 * MIB, transcendentals=0),
        name="offer",
    )(info, in_hbm(own), in_hbm(beside))


core_swap = functools.partial(lax.ppermute, axis_name="grp", perm=[(g, g ^ 1) for g in range(4)])
plane_swap = functools.partial(lax.ppermute, axis_name="grp", perm=[(g, g ^ 2) for g in range(4)])


def exchange_all(cache_t, info):
    across = plane_swap(cache_t)
    corner = core_swap(across)
    return jnp.where(info[3] == info[2] ^ 2, across, corner)


def tie(*trees):
    leaves, structure = jax.tree.flatten(trees)
    places = [at for at, leaf in enumerate(leaves) if isinstance(leaf, jax.Array)]
    held = lax.optimization_barrier([leaves[at] for at in places])
    for at, leaf in zip(places, held):
        leaves[at] = leaf
    return jax.tree.unflatten(structure, leaves)


def blank(like):
    return pl.pallas_call(
        lambda out_ref: None,
        out_shape=jax.ShapeDtypeStruct(like.shape, like.dtype),
        out_specs=whole(pl.ANY),
        compiler_params=pltpu.CompilerParams(vmem_limit_bytes=MIB),
        name="blank",
    )()


def body(cache, queries, new_latent, lengths, donor, value_up, out_proj):
    parts = lax.axis_size("ctx")
    steps, _, samples, heads, key_width = queries.shape
    latent = value_up.shape[1]
    cache_t = jnp.swapaxes(cache[0], 0, 1)
    local_len = cache_t.shape[1]
    info, crowded = plan(lengths, donor, local_len)
    fresh = new_latent.reshape(steps, samples, key_width)

    ring = list(range(0, parts, 2)) + list(range(parts - 1, 0, -2))
    to_right = [(ring[i], ring[(i + 1) % parts]) for i in range(parts)]
    to_left = [(b, a) for a, b in to_right]
    right = functools.partial(lax.ppermute, axis_name="ctx", perm=to_right)
    left = functools.partial(lax.ppermute, axis_name="ctx", perm=to_left)
    reach = parts // 2

    step_rows = samples * heads
    mine_rows = queries.reshape(steps * step_rows, key_width)
    rows, cut = steps * step_rows, HANDOVER * step_rows
    half = rows // 2 if rows % 32 == 0 else rows
    four = lax.axis_size("grp") == 4
    if four:
        beside = core_swap(cache_t)

    lefts, rights = [mine_rows], [mine_rows]

    def pieces_of(hop, start, stop):
        if hop == 0:
            return [(mine_rows, start, stop)]
        if hop < reach:
            return [(lefts[hop], start, stop), (rights[hop], start, stop)]
        found = []
        for block, first in ((lefts[hop], 0), (rights[hop], half)):
            low, high = max(start, first), min(stop, first + half)
            if low < high and block is not None:
                found.append((block, low - first, high - first))
        return found

    width = out_proj.shape[1]
    unit = width // 8 if width % 1024 == 0 else width
    loads = (2, 2)
    loaded = []

    def load_next(units):
        start = sum(piece.shape[1] for piece in loaded)
        stop = min(start + units * unit, width)
        return (out_proj, start, stop) if start < stop else None

    def attend_more(kinds, pieces, units, *rest):
        load = load_next(units)
        results = attend(kinds, pieces, [cache_t], info, 0, latent, *rest, load=load)
        if load:
            loaded.append(results.pop())
        return results

    def attend_early(hop):
        if hop == 0:
            return None
        kinds = ["ends"] if hop == reach else ["keep", "keep"]
        units = loads[hop - 1] if hop <= len(loads) else 0
        return attend_more(kinds, pieces_of(hop, 0, cut), units)

    early_parts = []
    for hop in range(1, reach + 1):
        if hop < reach:
            came = (right(lefts[-1]), left(rights[-1]))
        else:
            came = (
                right(lefts[-1][:half]),
                left(rights[-1][half:]) if half < rows else None,
            )
        extra = None
        if hop == 1 and four:
            extra = offer(info, cache_t, beside)
        elif hop == 2 and four:
            extra = lax.cond(
                crowded.reshape(()) != 0, exchange_all, lambda rows, _: blank(rows), cache_t, info
            )
        came, extra, parts_now = tie(came, extra, attend_early(hop - 1))
        if hop == 1 and four:
            far_half = plane_swap(extra)
        elif hop == 2 and four:
            spare = extra
        lefts.append(came[0])
        rights.append(came[1])
        early_parts.append(parts_now)
    early_parts.append(attend_early(reach))

    if four:
        far_half, lefts[reach] = tie(far_half, lefts[reach])
        moved = [cache_t, beside, far_half, core_swap(far_half), spare]
    else:
        shards = lax.all_gather(cache_t, "grp", axis=0, tiled=False)
        found = lax.dynamic_index_in_dim(shards, info[3], 0, keepdims=False)
        moved = [found, found, found[: key_width // 2], found[key_width // 2 :], found]
    near = reach - 1
    late_ends, *late_near, moved_rows = attend(
        ["ends", "keep", "keep"],
        pieces_of(reach, cut, rows) + pieces_of(near, cut, rows),
        moved,
        info,
        1,
        latent,
    )

    sections = tuple(range(sections_of(cut)))
    late_sections = tuple(range(sections_of(rows - cut)))

    def hop_back(going):
        return [
            [(send(block), cover) for block, cover in items]
            for send, items in zip((left, right), going)
        ]

    def merge_back(came, kept, sections):
        return [[(block, sections)] for block in merge(list(zip(came, kept)))]

    def ends_back(ends):
        return [[(ends[0], (0,))], [(ends[1], (1,))] if len(ends) > 1 else []]

    early_came = hop_back(ends_back(early_parts[reach][0]))
    early_came, late_ends, late_near = tie(early_came, late_ends, late_near)
    late_came = hop_back(ends_back(late_ends))
    early_came = hop_back(merge_back(early_came, early_parts[near], sections))
    kinds, pieces = ["own"], pieces_of(0, cut, rows)
    for hop in range(1, near):
        kinds += ["keep", "keep"]
        pieces += pieces_of(hop, cut, rows)
    results = attend(kinds, pieces, [moved_rows], info, 1, latent, fresh, (HANDOVER, heads))
    late_came, results = tie(late_came, results)
    late_came = hop_back(merge_back(late_came, late_near, late_sections))
    early_came, late_came = tie(early_came, late_came)

    early_parts[0] = attend_more(["own"], pieces_of(0, 0, cut), 2, fresh, (0, heads))
    late_parts = [[results[0]]]
    for hop in range(1, near):
        late_parts.append(results[2 * hop - 1 : 2 * hop + 1])
    for hop in range(near - 1, 0, -1):
        early_came = hop_back(merge_back(early_came, early_parts[hop], sections))
        late_came = hop_back(merge_back(late_came, late_parts[hop], late_sections))
        early_came, late_came, early_parts[0] = tie(early_came, late_came, early_parts[0])
    load = load_next(8)
    if load:
        loaded.append(load_alone(*load))
    finals = [
        (came[0][0][0], came[1][0][0], own[0])
        for came, own in ((early_came, early_parts[0]), (late_came, late_parts[0]))
    ]

    term = finish(finals, value_up, loaded, parts)
    shares = lax.all_to_all(term, "ctx", split_axis=0, concat_axis=0, tiled=True)
    mixed = jnp.sum(shares.astype(jnp.float32), axis=0).astype(jnp.bfloat16)
    return mixed.reshape(steps, 1, samples, mixed.shape[-1])


def solution(mesh):
    return jax.shard_map(
        body,
        mesh=mesh,
        in_specs=(
            P("grp", "ctx", None),
            P(None, "grp", None, "ctx", None),
            P(None, "grp", None, None),
            P(),
            P(),
            P("ctx", None, None),
            P("ctx", None),
        ),
        out_specs=P(None, "grp", None, "ctx"),
        check_vma=False,
    )
```
